512 devices in a mesh: tm: 32 (over z, x), rows: 16 (over y, core).
Axes of the slice: x: 4, y: 8, z: 8, core: 2. Of those that a mesh axis runs over, the one named last changes fastest.
Arguments:
- frames: bfloat16 [64, 128, 48, 128], P('tm', 'rows'), may hold values from -60 to 60
- lengths: int32 [8], replicated, may hold values from 1 to 16, as said below
- norm_gain_one: float32 [128], replicated, may hold values from 0.5 to 1.5
- norm_shift_one: float32 [128], replicated, may hold values from -0.5 to 0.5
- conv_one: bfloat16 [3, 3, 3, 128, 128], replicated, may hold values from -0.109375 to 0.109375
- bias_one: float32 [128], replicated, may hold values from -1 to 1
- norm_gain_two: float32 [128], replicated, may hold values from 0.5 to 1.5
- norm_shift_two: float32 [128], replicated, may hold values from -0.5 to 0.5
- conv_two: bfloat16 [3, 3, 3, 128, 128], replicated, may hold values from -0.109375 to 0.109375
- bias_two: float32 [128], replicated, may hold values from -1 to 1
Outputs:
- encoded: float32 [64, 128, 48, 128], P('tm', 'rows')
The draws below stay inside these ranges and needn't reach their ends.
Inputs may be any that keep to these rules, and one draw needn't show every extreme that they name: 8 video lengths that sum to 64; the longest has exactly 16 frames.
All inputs are finite; a program needn't handle non-finite values.
Results may differ from the reference program's by a relative error of at most 0.0014.
Values may be sent and summed in bfloat16 or wider, within the bound.
A program may use at most 64 MiB of HBM per device.

```python
import math
import jax
import jax.numpy as jnp
from jax import lax

CH = 128
GROUPS = 32
VIDEOS = 8
WIDTH = 48
FRAMES = 64
HEIGHT = 128
MOST = 16


def shared_lengths(key):
    key = jax.random.fold_in(key, 11)
    others = VIDEOS - 1
    weight_key, loop_key = jax.random.split(key)
    weights = jax.random.randint(weight_key, (others,), 1, 5, jnp.int32)
    indices = jnp.arange(others, dtype=jnp.int32)

    def add_frame(step, counts):
        step_key = jax.random.fold_in(loop_key, step)
        scores = jax.random.randint(step_key, (others,), 0, 1 << 16, jnp.int32) * weights
        scores = scores * others + indices
        scores = jnp.where(counts < MOST, scores, -1)
        picked = jnp.argmax(scores).astype(jnp.int32)
        return counts + (indices == picked).astype(jnp.int32)
    counts = lax.fori_loop(0, FRAMES - MOST - others, add_frame, jnp.ones((others,), jnp.int32))
    return jnp.concatenate([counts, jnp.full((1,), MOST, jnp.int32)]).astype(jnp.int32)


def draw_frames(key, part):
    lengths = shared_lengths(key)
    key = jax.random.fold_in(key, 5)
    key_rows, key_cols, key_base, key_amp, key_off = jax.random.split(key, 5)
    offsets = jnp.cumsum(lengths).astype(jnp.int32) - lengths
    frame_ids = jnp.arange(FRAMES, dtype=jnp.int32)
    video = (jnp.sum((offsets[None, :] <= frame_ids[:, None]).astype(jnp.int32), axis=1) - 1).astype(jnp.int32)
    position = (frame_ids - jnp.take(offsets, video)).astype(jnp.float32)
    span = jnp.maximum(jnp.take(lengths, video) - 1, 1).astype(jnp.float32)
    ramp = 0.2 + 0.8 * position / span
    amplitude = jnp.take(jax.random.uniform(key_amp, (VIDEOS,), jnp.float32, 0.25, 1.0), video) * ramp
    group_offset = jax.random.uniform(key_off, (VIDEOS, GROUPS), jnp.float32, -2.5, 2.5)
    frame_offset = jnp.repeat(jnp.take(group_offset, video, axis=0), CH // GROUPS, axis=1)
    row_scale = jnp.exp(jax.random.uniform(key_rows, (HEIGHT,), jnp.float32, 0.0, 0.5 * math.log(10.0)))
    col_scale = jnp.exp(jax.random.uniform(key_cols, (WIDTH,), jnp.float32, 0.0, 0.5 * math.log(10.0)))
    scale = row_scale[None, :, None, None] * col_scale[None, None, :, None]
    base = jnp.clip(jax.random.normal(key_base, (FRAMES, HEIGHT, WIDTH, CH), jnp.float32), -6.0, 6.0)
    values = 0.9 * base * scale * amplitude[:, None, None, None] + frame_offset[:, None, None, :]
    return values.astype(jnp.bfloat16)


def draw_lengths(key, part):
    return shared_lengths(key)


def bell_draw(rng, shape, spread, reach, held_as=jnp.bfloat16):
    return jnp.clip(spread * jax.random.normal(rng, shape, jnp.float32), -reach, reach).astype(held_as)


def setup_inputs(seed: int = 0) -> dict:
    key_list = jax.random.split(jax.random.key(seed), 11)
    frames = draw_frames(jax.random.fold_in(key_list[10], 71), 0)
    lengths = draw_lengths(jax.random.fold_in(key_list[10], 71), 0)
    norm_gain_one = jnp.clip(jax.random.uniform(key_list[2], (CH,), jnp.float32, 0.5, 1.5), 0.5, 1.5)
    norm_shift_one = jnp.clip(jax.random.uniform(key_list[3], (CH,), jnp.float32, -0.5, 0.5), -0.5, 0.5)
    conv_one = bell_draw(key_list[4], (3, 3, 3, CH, CH), (27 * CH) ** -0.5, 0.109375)
    bias_one = jnp.clip(jax.random.uniform(key_list[5], (CH,), jnp.float32, -1.0, 1.0), -1.0, 1.0)
    norm_gain_two = jnp.clip(jax.random.uniform(key_list[6], (CH,), jnp.float32, 0.5, 1.5), 0.5, 1.5)
    norm_shift_two = jnp.clip(jax.random.uniform(key_list[7], (CH,), jnp.float32, -0.5, 0.5), -0.5, 0.5)
    conv_two = bell_draw(key_list[8], (3, 3, 3, CH, CH), (27 * CH) ** -0.5, 0.109375)
    bias_two = jnp.clip(jax.random.uniform(key_list[9], (CH,), jnp.float32, -1.0, 1.0), -1.0, 1.0)
    return dict(frames=frames, lengths=lengths, norm_gain_one=norm_gain_one, norm_shift_one=norm_shift_one, conv_one=conv_one, bias_one=bias_one, norm_gain_two=norm_gain_two, norm_shift_two=norm_shift_two, conv_two=conv_two, bias_two=bias_two)


def plan_frames(lengths):
    offsets = jnp.cumsum(lengths).astype(jnp.int32) - lengths
    frame_ids = jnp.arange(FRAMES, dtype=jnp.int32)
    inside = offsets[None, :] <= frame_ids[:, None]
    video = lax.optimization_barrier(jnp.sum(inside.astype(jnp.int32), axis=1)) - 1
    starts = lax.optimization_barrier(jnp.max(jnp.where(inside, offsets[None, :], 0), axis=1)).astype(jnp.int32)
    onehot = (video[:, None] == jnp.arange(VIDEOS, dtype=jnp.int32)[None, :]).astype(jnp.float32)
    taps = [jnp.maximum(frame_ids - back, starts).astype(jnp.int32) for back in (2, 1, 0)]
    return (onehot, taps)

def group_norm(values, onehot, counts, gain, shift):
    per_group = lax.optimization_barrier(jnp.sum(values, axis=(1, 2))).reshape(FRAMES, GROUPS, CH // GROUPS).sum(-1)
    mean = jnp.dot(onehot.T, per_group, precision=lax.Precision.HIGHEST) / counts[:, None]
    frame_mean = jnp.repeat(jnp.dot(onehot, mean, precision=lax.Precision.HIGHEST), CH // GROUPS, axis=1)
    centered = values - frame_mean[:, None, None, :]
    squares = lax.optimization_barrier(jnp.sum(centered * centered, axis=(1, 2))).reshape(FRAMES, GROUPS, CH // GROUPS).sum(-1)
    var = jnp.dot(onehot.T, squares, precision=lax.Precision.HIGHEST) / counts[:, None]
    scale = jnp.repeat(jnp.dot(onehot, lax.rsqrt(var + 1e-06), precision=lax.Precision.HIGHEST), CH // GROUPS, axis=1)
    return centered * scale[:, None, None, :] * gain + shift

def causal_conv(act, weight, bias, taps):
    total = jnp.zeros((FRAMES, HEIGHT, WIDTH, CH), jnp.float32)
    for step in range(3):
        picked = jnp.take(act, taps[step], axis=0).astype(jnp.float32)
        total = total + lax.conv_general_dilated(picked, weight[step].astype(jnp.float32), (1, 1), 'SAME', dimension_numbers=('NHWC', 'HWIO', 'NHWC'), precision=lax.Precision.HIGHEST)
    return total + bias

def reference(frames, lengths, norm_gain_one, norm_shift_one, conv_one, bias_one, norm_gain_two, norm_shift_two, conv_two, bias_two):
    onehot, taps = plan_frames(lengths)
    counts = lengths.astype(jnp.float32) * (HEIGHT * WIDTH * (CH // GROUPS))
    values = frames.astype(jnp.float32)
    act_one = jax.nn.silu(group_norm(values, onehot, counts, norm_gain_one, norm_shift_one)).astype(jnp.bfloat16)
    middle = causal_conv(act_one, conv_one, bias_one, taps).astype(jnp.bfloat16)
    act_two = jax.nn.silu(group_norm(middle.astype(jnp.float32), onehot, counts, norm_gain_two, norm_shift_two)).astype(jnp.bfloat16)
    return values + causal_conv(act_two, conv_two, bias_two, taps)
```

```python
import functools

import jax
import jax.numpy as jnp
from jax import lax
from jax.experimental import pallas as pl
from jax.experimental.pallas import tpu as pltpu
from jax.sharding import PartitionSpec as P

GROUPS = 32
MOST = 16
MESH = pl.DeviceIdType.MESH


def tm_offsets(n_tm, count):
    reach = -(-(MOST - 1) // count)
    if 2 * reach + 1 >= n_tm:
        return list(range(n_tm))
    return list(range(reach + 1)) + [-d for d in range(1, reach + 1)]


def wrapped(index, offset, size):
    return lax.rem(index + (offset + size), size)


def group_total(row, width):
    lane = lax.broadcasted_iota(jnp.int32, row.shape, 1)
    channels = row.shape[1]
    span = 1
    while span < width:
        ahead = pltpu.roll(row, channels - span, 1)
        behind = pltpu.roll(row, span, 1)
        row = row + jnp.where((lane // span) % 2 == 0, ahead, behind)
        span *= 2
    return row


def kernel(
    n_tm, n_rows,
    frames, lengths, gain_one, shift_one, conv_one, bias_one, gain_two, shift_two, conv_two, bias_two,
    out,
    raw, mid, act, taps_one, taps_two, vecs, lens, rows_one, rows_two, tms_one, tms_two, result,
    load_sem, halo_send, halo_recv, stat_send, stat_recv, out_sem,
):
    count, height, cols, width = frames.shape
    videos = lengths.shape[0]
    tm = lax.axis_index("tm")
    row = lax.axis_index("rows")
    first = tm * count
    offsets = tm_offsets(n_tm, count)

    load_frames = pltpu.make_async_copy(
        frames, raw.at[pl.ds(count, count), pl.ds(1, height)], load_sem.at[0]
    )
    load_frames.start()
    load_lens = pltpu.make_async_copy(lengths, lens, load_sem.at[1])
    load_lens.start()
    load_vecs = []
    for i, vec in enumerate((gain_one, shift_one, bias_one, gain_two, shift_two, bias_two)):
        load_vecs.append(pltpu.make_async_copy(vec, vecs.at[i], load_sem.at[2 + i]))
    load_one, load_two = [], []
    for dx in range(3):
        load_one.append(
            pltpu.make_async_copy(
                conv_one.at[:, :, dx], taps_one.at[:, :, :, pl.ds(dx * width, width)], load_sem.at[8 + dx]
            )
        )
        load_two.append(
            pltpu.make_async_copy(
                conv_two.at[:, :, dx], taps_two.at[:, :, :, pl.ds(dx * width, width)], load_sem.at[11 + dx]
            )
        )

    peers = [(0, k) for k in range(1, n_rows)]
    peers += [(d, 0) for d in offsets[1:]]
    peers += [(d, k) for d in (1, -1) for k in (1, -1)]
    barrier = pltpu.get_barrier_semaphore()
    for d, k in peers:
        pl.semaphore_signal(
            barrier,
            inc=1,
            device_id={"tm": wrapped(tm, d, n_tm), "rows": wrapped(row, k, n_rows)},
            device_id_type=MESH,
        )
    for load in load_vecs + load_one + load_two:
        load.start()

    def halo_copies(block, half):
        own = pl.ds(count, count)
        prior = pl.ds(0, count)
        plans = [
            (block.at[own, pl.ds(1, height)], block.at[prior, pl.ds(1, height)], 1, 0),
            (block.at[own, pl.ds(height, 1)], block.at[own, pl.ds(0, 1)], 0, 1),
            (block.at[own, pl.ds(1, 1)], block.at[own, pl.ds(height + 1, 1)], 0, -1),
            (block.at[own, pl.ds(height, 1)], block.at[prior, pl.ds(0, 1)], 1, 1),
            (block.at[own, pl.ds(1, 1)], block.at[prior, pl.ds(height + 1, 1)], 1, -1),
        ]
        return [
            pltpu.make_async_remote_copy(
                src_ref=src,
                dst_ref=dst,
                send_sem=halo_send.at[half, i],
                recv_sem=halo_recv.at[half, i],
                device_id={"tm": wrapped(tm, d, n_tm), "rows": wrapped(row, k, n_rows)},
                device_id_type=MESH,
            )
            for i, (src, dst, d, k) in enumerate(plans)
        ]

    def spread(slots, steps, sem):
        for i, (d, k) in enumerate(steps):
            pltpu.make_async_remote_copy(
                src_ref=slots.at[0],
                dst_ref=slots.at[1 + i],
                send_sem=stat_send.at[sem],
                recv_sem=stat_recv.at[sem],
                device_id={"tm": wrapped(tm, d, n_tm), "rows": wrapped(row, k, n_rows)},
                device_id_type=MESH,
            ).start()

    def whole(slots, steps, sem):
        others = slots.at[pl.ds(1, len(steps))]
        return pltpu.make_async_remote_copy(
            src_ref=others,
            dst_ref=others,
            send_sem=stat_send.at[sem],
            recv_sem=stat_recv.at[sem],
            device_id={"tm": wrapped(tm, 1, n_tm), "rows": row},
            device_id_type=MESH,
        )

    row_steps = [(0, k) for k in range(1, n_rows)]
    tm_steps = [(d, 0) for d in offsets[1:]]
    per_block = float(height * cols)
    per_frame = per_block * n_rows

    def local_stats(block):
        sums, squares = [], []
        for f in range(count):
            values = block[count + f, 1 : height + 1].reshape(height * cols, width).astype(jnp.float32)
            total = jnp.sum(values, axis=0, keepdims=True)
            off = values - total * (1.0 / per_block)
            sums.append(total)
            squares.append(jnp.sum(off * off, axis=0, keepdims=True))
        return jnp.concatenate(sums + squares + [jnp.zeros((8 - 2 * count, width), jnp.float32)], axis=0)

    def merged_rows(slots):
        parts = slots[...]
        total = jnp.sum(parts, axis=0)
        off = parts * (1.0 / per_block) - (total * (1.0 / per_frame))[None]
        between = jnp.sum(off * off, axis=0) * per_block
        return jnp.concatenate(
            [
                total[:count],
                total[count : 2 * count] + between[:count],
                jnp.zeros((8 - 2 * count, width), jnp.float32),
            ],
            axis=0,
        )

    def merged_frames(slots, inside, length):
        parts = slots[...]
        total = jnp.sum(jnp.where(inside, parts, 0.0), axis=0)
        entries = length.astype(jnp.float32) * (per_frame * (width // GROUPS))
        mean = group_total(jnp.sum(total[:count], axis=0, keepdims=True), width // GROUPS) / entries
        off = parts * (1.0 / per_frame) - mean[None]
        between = jnp.sum(jnp.where(inside, off * off, 0.0), axis=0) * per_frame
        squares = jnp.sum(total[count : 2 * count] + between[:count], axis=0, keepdims=True)
        var = group_total(squares, width // GROUPS) / entries
        return mean, lax.rsqrt(var + 1e-6)

    def activate(block, stats, gain, shift):
        top = row == 0
        bottom = row == n_rows - 1
        for f in range(2 * count):
            mean, scale = stats[max(f - count, 0)]
            factor = scale * gain
            for i in range(height + 2):
                v = (block[f, i].astype(jnp.float32) - mean) * factor + shift
                v = v * (0.5 * jnp.tanh(0.5 * v) + 0.5)
                if i == 0:
                    v = jnp.where(top, 0.0, v)
                if i == height + 1:
                    v = jnp.where(bottom, 0.0, v)
                act[f, i] = v.astype(jnp.bfloat16)

    def conv(taps, sources):
        lefts = []
        for f in range(count):
            pieces = []
            for dt in range(3):
                for dy in range(3):
                    pieces.append(
                        act[sources[f][dt], dy : dy + height].reshape(height * cols, width)
                    )
            lefts.append(jnp.concatenate(pieces, axis=1))
        left = jnp.concatenate(lefts, axis=0)
        right = taps[...].reshape(9 * width, 3 * width)
        return jnp.dot(left, right, preferred_element_type=jnp.float32)

    column = lax.broadcasted_iota(jnp.int32, (cols, width), 0)

    def joined(wide, i):
        y = wide[i * cols : (i + 1) * cols]
        before = pltpu.roll(y[:, :width], 1, 0)
        after = pltpu.roll(y[:, 2 * width :], cols - 1, 0)
        return (
            y[:, width : 2 * width]
            + jnp.where(column == 0, 0.0, before)
            + jnp.where(column == cols - 1, 0.0, after)
        )

    load_frames.wait()
    rows_one[0] = local_stats(raw)
    pl.semaphore_wait(barrier, len(peers))
    spread(rows_one, row_steps, 0)
    halo_one = halo_copies(raw, 0)
    for copy in halo_one:
        copy.start()

    load_lens.wait()
    starts, stops = [], []
    for f in range(count):
        start = jnp.int32(0)
        stop = jnp.int32(0)
        offset = jnp.int32(0)
        for v in range(videos):
            size = lens[v]
            here = offset <= first + f
            start = jnp.where(here, offset, start)
            stop = jnp.where(here, offset + size, stop)
            offset = offset + size
        starts.append(start)
        stops.append(stop)
    slot = lax.broadcasted_iota(jnp.int32, tms_one.shape, 0)
    part = lax.broadcasted_iota(jnp.int32, tms_one.shape, 1)
    reach = max(offsets)
    base = first - count * jnp.where(slot <= reach, slot, reach - slot)
    base = jnp.where(base < 0, base + count * n_tm, base)
    base = jnp.where(base >= count * n_tm, base - count * n_tm, base)
    frame = base + lax.rem(part, count)
    inside = [(frame >= starts[f]) & (frame < stops[f]) for f in range(count)]
    sources = [
        [jnp.maximum(f + dt, starts[f] - first + 2) for dt in range(3)] for f in range(count)
    ]

    whole(rows_one, row_steps, 0).wait_recv()
    tms_one[0] = merged_rows(rows_one)
    spread(tms_one, tm_steps, 1)
    for load in load_vecs:
        load.wait()
    whole(tms_one, tm_steps, 1).wait_recv()
    stats = [merged_frames(tms_one, inside[f], stops[f] - starts[f]) for f in range(count)]
    for copy in halo_one:
        copy.wait_recv()
    activate(raw, stats, vecs[0:1], vecs[1:2])
    for load in load_one:
        load.wait()
    wide = conv(taps_one, sources)
    for f in range(count):
        for i in range(height):
            mid[count + f, 1 + i] = (joined(wide, f * height + i) + vecs[2:3]).astype(jnp.bfloat16)

    rows_two[0] = local_stats(mid)
    spread(rows_two, row_steps, 2)
    halo_two = halo_copies(mid, 1)
    for copy in halo_two:
        copy.start()
    whole(rows_two, row_steps, 2).wait_recv()
    tms_two[0] = merged_rows(rows_two)
    spread(tms_two, tm_steps, 3)
    whole(tms_two, tm_steps, 3).wait_recv()
    stats = [merged_frames(tms_two, inside[f], stops[f] - starts[f]) for f in range(count)]
    for copy in halo_two:
        copy.wait_recv()
    activate(mid, stats, vecs[3:4], vecs[4:5])
    for load in load_two:
        load.wait()
    wide = conv(taps_two, sources)
    stores = []
    for f in range(count):
        for i in range(height):
            result[f, i] = (
                joined(wide, f * height + i) + vecs[5:6] + raw[count + f, 1 + i].astype(jnp.float32)
            )
        stores.append(pltpu.make_async_copy(result.at[f], out.at[f], out_sem.at[f]))
        stores[-1].start()

    for copy in halo_one + halo_two:
        copy.wait_send()
    whole(rows_one, row_steps, 0).wait_send()
    whole(tms_one, tm_steps, 1).wait_send()
    whole(rows_two, row_steps, 2).wait_send()
    whole(tms_two, tm_steps, 3).wait_send()
    for store in stores:
        store.wait()


def per_device(n_tm, n_rows, *args):
    frames, lengths = args[0], args[1]
    count, height, cols, width = frames.shape
    window = len(tm_offsets(n_tm, count))
    block = pltpu.VMEM((2 * count, height + 2, cols, width), jnp.bfloat16)
    taps = pltpu.VMEM((3, 3, width, 3 * width), jnp.bfloat16)
    return pl.pallas_call(
        functools.partial(kernel, n_tm, n_rows),
        out_shape=jax.ShapeDtypeStruct(frames.shape, jnp.float32),
        in_specs=[pl.BlockSpec(memory_space=pl.ANY)] * len(args),
        out_specs=pl.BlockSpec(memory_space=pl.ANY),
        scratch_shapes=[
            block, block, block, taps, taps,
            pltpu.VMEM((8, width), jnp.float32),
            pltpu.SMEM(lengths.shape, jnp.int32),
            pltpu.VMEM((n_rows, 8, width), jnp.float32),
            pltpu.VMEM((n_rows, 8, width), jnp.float32),
            pltpu.VMEM((window, 8, width), jnp.float32),
            pltpu.VMEM((window, 8, width), jnp.float32),
            pltpu.VMEM(frames.shape, jnp.float32),
            pltpu.SemaphoreType.DMA((14,)),
            pltpu.SemaphoreType.DMA((2, 5)),
            pltpu.SemaphoreType.DMA((2, 5)),
            pltpu.SemaphoreType.DMA((4,)),
            pltpu.SemaphoreType.DMA((4,)),
            pltpu.SemaphoreType.DMA((count,)),
        ],
        compiler_params=pltpu.CompilerParams(
            collective_id=0, has_side_effects=True, vmem_limit_bytes=63 * 1024 * 1024
        ),
        name="residual_block",
    )(*args)


def solution(mesh):
    placed = (P("tm", "rows", None, None), P(), P(), P(), P(), P(), P(), P(), P(), P())
    return jax.shard_map(
        functools.partial(per_device, mesh.shape["tm"], mesh.shape["rows"]),
        mesh=mesh,
        in_specs=placed,
        out_specs=P("tm", "rows", None, None),
        check_vma=False,
    )
```

```python
import functools

import jax
import jax.numpy as jnp
from jax import lax
from jax.experimental import pallas as pl
from jax.experimental.pallas import tpu as pltpu
from jax.sharding import PartitionSpec as P

GROUPS = 32
MOST = 16
MESH = pl.DeviceIdType.MESH


def tm_offsets(n_tm, count):
    reach = min(-(-(MOST - 1) // count), n_tm - 1)
    return [d for far in range(1, reach + 1) for d in (far, -far)]


def wrapped(index, offset, size):
    return lax.rem(index + (offset + size), size)


def group_total(row, width):
    lane = lax.broadcasted_iota(jnp.int32, row.shape, 1)
    channels = row.shape[1]
    span = 1
    while span < width:
        ahead = pltpu.roll(row, channels - span, 1)
        behind = pltpu.roll(row, span, 1)
        row = row + jnp.where((lane // span) % 2 == 0, ahead, behind)
        span *= 2
    return row


def kernel(
    n_tm, n_rows,
    frames, lengths, gain_one, shift_one, conv_one, bias_one, gain_two, shift_two, conv_two, bias_two,
    out,
    raw, mid, act, taps_one, taps_two, vecs, lens, rows_one, rows_two, tms_one, tms_two, result,
    load_sem, halo_send, halo_recv, row_send, row_recv, tm_send, tm_recv, out_sem,
):
    count, height, cols, width = frames.shape
    videos = lengths.shape[0]
    tm = lax.axis_index("tm")
    row = lax.axis_index("rows")
    first = tm * count
    offsets = tm_offsets(n_tm, count)

    load_frames = pltpu.make_async_copy(
        frames, raw.at[pl.ds(count, count), pl.ds(1, height)], load_sem.at[0]
    )
    load_frames.start()

    def exists(d):
        return (tm + d >= 0) & (tm + d < n_tm)

    def device(d, k):
        return {"tm": tm + d, "rows": wrapped(row, k, n_rows)}

    barrier = pltpu.get_barrier_semaphore()
    for k in range(1, n_rows):
        pl.semaphore_signal(barrier, inc=1, device_id=device(0, k), device_id_type=MESH)
    expected = n_rows - 1
    for d in sorted(offsets, key=abs, reverse=True):
        present = exists(d)
        steps = (0, 1, -1) if abs(d) == 1 else (0,)
        expected = expected + jnp.where(present, len(steps), 0)

        @pl.when(present)
        def _(d=d, steps=steps):
            for k in steps:
                pl.semaphore_signal(barrier, inc=1, device_id=device(d, k), device_id_type=MESH)

    load_lens = pltpu.make_async_copy(lengths, lens, load_sem.at[1])
    load_lens.start()
    load_vecs = []
    for i, vec in enumerate((gain_one, shift_one, bias_one, gain_two, shift_two, bias_two)):
        load_vecs.append(pltpu.make_async_copy(vec, vecs.at[i], load_sem.at[2 + i]))
    load_one, load_two = [], []
    for dx in range(3):
        load_one.append(
            pltpu.make_async_copy(
                conv_one.at[:, :, dx], taps_one.at[:, :, :, pl.ds(dx * width, width)], load_sem.at[8 + dx]
            )
        )
        load_two.append(
            pltpu.make_async_copy(
                conv_two.at[:, :, dx], taps_two.at[:, :, :, pl.ds(dx * width, width)], load_sem.at[11 + dx]
            )
        )
    for load in load_vecs + load_one + load_two:
        load.start()

    class Halo:
        def __init__(self, block, half):
            own, prior = pl.ds(count, count), pl.ds(0, count)
            whole, last, head = pl.ds(1, height), pl.ds(height, 1), pl.ds(1, 1)
            above, below = pl.ds(0, 1), pl.ds(height + 1, 1)
            plans = [
                (own, last, own, above, 0, 1),
                (own, head, own, below, 0, -1),
                (own, last, prior, above, 1, 1),
                (own, head, prior, below, 1, -1),
                (own, whole, prior, whole, 1, 0),
            ]
            copies = [
                pltpu.make_async_remote_copy(
                    src_ref=block.at[f, src],
                    dst_ref=block.at[g, dst],
                    send_sem=halo_send.at[half, i],
                    recv_sem=halo_recv.at[half, i],
                    device_id=device(d, k),
                    device_id_type=MESH,
                )
                for i, (f, src, g, dst, d, k) in enumerate(plans)
            ]
            self.beside, self.onward = copies[:2], copies[2:]

        def start(self):
            for copy in self.beside:
                copy.start()

            @pl.when(exists(1))
            def _():
                for copy in self.onward:
                    copy.start()

        def wait_recv(self):
            for copy in self.beside:
                copy.wait_recv()

            @pl.when(exists(-1))
            def _():
                for copy in self.onward:
                    copy.wait_recv()

        def wait_send(self):
            for copy in self.beside:
                copy.wait_send()

            @pl.when(exists(1))
            def _():
                for copy in self.onward:
                    copy.wait_send()

    class Rows:
        def __init__(self, slots, half):
            self.copies = [
                pltpu.make_async_remote_copy(
                    src_ref=slots.at[pl.ds(0, 1)],
                    dst_ref=slots.at[pl.ds(k, 1)],
                    send_sem=row_send.at[half, k],
                    recv_sem=row_recv.at[half, k],
                    device_id=device(0, k),
                    device_id_type=MESH,
                )
                for k in range(1, n_rows)
            ]

        def start(self):
            for copy in self.copies:
                copy.start()

        def wait_recv(self):
            for copy in self.copies:
                copy.wait_recv()

        def wait_send(self):
            for copy in self.copies:
                copy.wait_send()

    class Frames:
        def __init__(self, slots, half):
            self.copies = [
                pltpu.make_async_remote_copy(
                    src_ref=slots.at[pl.ds(0, 1)],
                    dst_ref=slots.at[pl.ds(1 + i, 1)],
                    send_sem=tm_send.at[half, i],
                    recv_sem=tm_recv.at[half, i],
                    device_id=device(d, 0),
                    device_id_type=MESH,
                )
                for i, d in enumerate(offsets)
            ]

        def start(self):
            for copy, d in zip(self.copies, offsets):
                pl.when(exists(d))(copy.start)

        def wait_recv(self):
            for copy, d in zip(self.copies, offsets):
                pl.when(exists(-d))(copy.wait_recv)

        def wait_send(self):
            for copy, d in zip(self.copies, offsets):
                pl.when(exists(d))(copy.wait_send)

    members = width // GROUPS
    per_block = float(height * cols * members)
    per_frame = per_block * n_rows
    quarter = lax.rem(lax.broadcasted_iota(jnp.int32, (1, width), 1), 2 * count)

    def local_stats(block):
        packed = jnp.zeros((1, width), jnp.float32)
        for f in range(count):
            values = block[count + f, 1 : height + 1].reshape(height * cols, width).astype(jnp.float32)
            total = jnp.sum(values, axis=0, keepdims=True)
            mean = total * (members / per_block)
            off = values - mean
            squares = jnp.sum(off * off, axis=0, keepdims=True)
            total = group_total(total, members)
            off = mean - total * (1.0 / per_block)
            squares = group_total(squares + off * off * (per_block / members), members)
            packed = jnp.where(quarter == f, total, packed)
            packed = jnp.where(quarter == count + f, squares, packed)
        return packed

    def merged_rows(slots):
        parts = slots[...]
        total = jnp.sum(parts, axis=0, keepdims=True)
        off = parts * (1.0 / per_block) - total * (1.0 / per_frame)
        between = jnp.sum(off * off, axis=0, keepdims=True) * per_block
        return total + jnp.where(quarter < count, 0.0, pltpu.roll(between, count, 1))

    def merged_frames(slots, inside, length):
        parts = slots[...]
        total = jnp.sum(jnp.where(inside, parts, 0.0), axis=0, keepdims=True)
        entries = length.astype(jnp.float32) * per_frame
        mean = group_total(jnp.where(quarter < count, total, 0.0), members) / entries
        off = parts * (1.0 / per_frame) - mean
        between = jnp.sum(jnp.where(inside, off * off, 0.0), axis=0, keepdims=True) * per_frame
        var = group_total(jnp.where(quarter < count, between, total), members) / entries
        return mean, lax.rsqrt(var + 1e-6)

    def activate(block, stats, gain, shift):
        top = row == 0
        bottom = row == n_rows - 1
        for f in range(2 * count):
            mean, scale = stats[max(f - count, 0)]
            factor = scale * gain
            for i in range(height + 2):
                v = (block[f, i].astype(jnp.float32) - mean) * factor + shift
                v = v * (0.5 * jnp.tanh(0.5 * v) + 0.5)
                if i == 0:
                    v = jnp.where(top, 0.0, v)
                if i == height + 1:
                    v = jnp.where(bottom, 0.0, v)
                act[f, i] = v.astype(jnp.bfloat16)

    def conv(taps, sources):
        lefts = []
        for f in range(count):
            pieces = []
            for dt in range(3):
                for dy in range(3):
                    pieces.append(
                        act[sources[f][dt], dy : dy + height].reshape(height * cols, width)
                    )
            lefts.append(jnp.concatenate(pieces, axis=1))
        left = jnp.concatenate(lefts, axis=0)
        right = taps[...].reshape(9 * width, 3 * width)
        return jnp.dot(left, right, preferred_element_type=jnp.float32)

    column = lax.broadcasted_iota(jnp.int32, (cols, width), 0)

    def joined(wide, i):
        y = wide[i * cols : (i + 1) * cols]
        before = pltpu.roll(y[:, :width], 1, 0)
        after = pltpu.roll(y[:, 2 * width :], cols - 1, 0)
        return (
            y[:, width : 2 * width]
            + jnp.where(column == 0, 0.0, before)
            + jnp.where(column == cols - 1, 0.0, after)
        )

    load_frames.wait()
    rows_one[pl.ds(0, 1)] = local_stats(raw)
    pl.semaphore_wait(barrier, expected)
    row_sums = Rows(rows_one, 0)
    row_sums.start()
    halo_one = Halo(raw, 0)
    halo_one.start()

    load_lens.wait()
    starts, stops = [], []
    for f in range(count):
        start = jnp.int32(0)
        stop = jnp.int32(0)
        offset = jnp.int32(0)
        for v in range(videos):
            size = lens[v]
            here = offset <= first + f
            start = jnp.where(here, offset, start)
            stop = jnp.where(here, offset + size, stop)
            offset = offset + size
        starts.append(start)
        stops.append(stop)
    slot = lax.broadcasted_iota(jnp.int32, tms_one.shape, 0)
    lane = lax.broadcasted_iota(jnp.int32, tms_one.shape, 1)
    far = (slot + 1) // 2
    home = tm - jnp.where(lax.rem(slot, 2) == 1, far, -far)
    frame = home * count + lax.rem(lane, count)
    known = slot <= len(offsets)
    inside = [known & (frame >= starts[f]) & (frame < stops[f]) for f in range(count)]
    sources = [
        [jnp.maximum(f + dt, starts[f] - first + 2) for dt in range(3)] for f in range(count)
    ]

    row_sums.wait_recv()
    tms_one[pl.ds(0, 1)] = merged_rows(rows_one)
    tm_sums = Frames(tms_one, 0)
    tm_sums.start()
    for load in load_vecs:
        load.wait()
    tm_sums.wait_recv()
    stats = [merged_frames(tms_one, inside[f], stops[f] - starts[f]) for f in range(count)]
    halo_one.wait_recv()
    activate(raw, stats, vecs[0:1], vecs[1:2])
    for load in load_one:
        load.wait()
    wide = conv(taps_one, sources)
    for f in range(count):
        for i in range(height):
            mid[count + f, 1 + i] = (joined(wide, f * height + i) + vecs[2:3]).astype(jnp.bfloat16)
    row_sums.wait_send()
    tm_sums.wait_send()
    halo_one.wait_send()

    rows_two[pl.ds(0, 1)] = local_stats(mid)
    row_sums = Rows(rows_two, 1)
    row_sums.start()
    halo_two = Halo(mid, 1)
    halo_two.start()
    row_sums.wait_recv()
    tms_two[pl.ds(0, 1)] = merged_rows(rows_two)
    tm_sums = Frames(tms_two, 1)
    tm_sums.start()
    tm_sums.wait_recv()
    stats = [merged_frames(tms_two, inside[f], stops[f] - starts[f]) for f in range(count)]
    halo_two.wait_recv()
    activate(mid, stats, vecs[3:4], vecs[4:5])
    for load in load_two:
        load.wait()
    wide = conv(taps_two, sources)
    stores = []
    for f in range(count):
        for i in range(height):
            result[f, i] = (
                joined(wide, f * height + i) + vecs[5:6] + raw[count + f, 1 + i].astype(jnp.float32)
            )
        stores.append(pltpu.make_async_copy(result.at[f], out.at[f], out_sem.at[f]))
        stores[-1].start()
    row_sums.wait_send()
    tm_sums.wait_send()
    halo_two.wait_send()
    for store in stores:
        store.wait()


def per_device(n_tm, n_rows, *args):
    frames, lengths = args[0], args[1]
    count, height, cols, width = frames.shape
    near = len(tm_offsets(n_tm, count))
    window = -(-(1 + near) // 8) * 8
    block = pltpu.VMEM((2 * count, height + 2, cols, width), jnp.bfloat16)
    taps = pltpu.VMEM((3, 3, width, 3 * width), jnp.bfloat16)
    return pl.pallas_call(
        functools.partial(kernel, n_tm, n_rows),
        out_shape=jax.ShapeDtypeStruct(frames.shape, jnp.float32),
        in_specs=[pl.BlockSpec(memory_space=pl.ANY)] * len(args),
        out_specs=pl.BlockSpec(memory_space=pl.ANY),
        scratch_shapes=[
            block, block, block, taps, taps,
            pltpu.VMEM((8, width), jnp.float32),
            pltpu.SMEM(lengths.shape, jnp.int32),
            pltpu.VMEM((n_rows, width), jnp.float32),
            pltpu.VMEM((n_rows, width), jnp.float32),
            pltpu.VMEM((window, width), jnp.float32),
            pltpu.VMEM((window, width), jnp.float32),
            pltpu.VMEM(frames.shape, jnp.float32),
            pltpu.SemaphoreType.DMA((14,)),
            pltpu.SemaphoreType.DMA((2, 5)),
            pltpu.SemaphoreType.DMA((2, 5)),
            pltpu.SemaphoreType.DMA((2, n_rows)),
            pltpu.SemaphoreType.DMA((2, n_rows)),
            pltpu.SemaphoreType.DMA((2, near)),
            pltpu.SemaphoreType.DMA((2, near)),
            pltpu.SemaphoreType.DMA((count,)),
        ],
        compiler_params=pltpu.CompilerParams(
            collective_id=0, has_side_effects=True, vmem_limit_bytes=63 * 1024 * 1024
        ),
        name="residual_block",
    )(*args)


def solution(mesh):
    placed = (P("tm", "rows", None, None), P(), P(), P(), P(), P(), P(), P(), P(), P())
    return jax.shard_map(
        functools.partial(per_device, mesh.shape["tm"], mesh.shape["rows"]),
        mesh=mesh,
        in_specs=placed,
        out_specs=P("tm", "rows", None, None),
        check_vma=False,
    )
```

```python
import functools

import jax
import jax.numpy as jnp
from jax import lax
from jax.experimental import pallas as pl
from jax.experimental.pallas import tpu as pltpu
from jax.sharding import PartitionSpec as P

GROUPS = 32
MOST = 16
MESH = pl.DeviceIdType.MESH


def tm_offsets(n_tm, count):
    reach = min(-(-(MOST - 1) // count), n_tm - 1)
    return [d for far in range(1, reach + 1) for d in (far, -far)]


def wrapped(index, offset, size):
    return lax.rem(index + (offset + size), size)


def group_total(row, width):
    lane = lax.broadcasted_iota(jnp.int32, row.shape, 1)
    channels = row.shape[1]
    span = 1
    while span < width:
        ahead = pltpu.roll(row, channels - span, 1)
        behind = pltpu.roll(row, span, 1)
        row = row + jnp.where((lane // span) % 2 == 0, ahead, behind)
        span *= 2
    return row


def kernel(
    n_tm, n_rows,
    frames, lengths, gain_one, shift_one, conv_one, bias_one, gain_two, shift_two, conv_two, bias_two,
    out,
    raw, mid, act, taps_one, taps_two, vecs, lens, rows_one, rows_two, tms_one, tms_two,
    load_sem, halo_send, halo_recv, row_send, row_recv, tm_send, tm_recv,
):
    count, height, cols, width = frames.shape
    videos = lengths.shape[0]
    tm = lax.axis_index("tm")
    row = lax.axis_index("rows")
    first = tm * count
    offsets = tm_offsets(n_tm, count)

    load_frames = pltpu.make_async_copy(
        frames, raw.at[pl.ds(count, count), pl.ds(1, height)], load_sem.at[0]
    )
    load_frames.start()

    def exists(d):
        return (tm + d >= 0) & (tm + d < n_tm)

    def device(d, k):
        return {"tm": tm + d, "rows": wrapped(row, k, n_rows)}

    barrier = pltpu.get_barrier_semaphore()
    for k in range(1, n_rows):
        pl.semaphore_signal(barrier, inc=1, device_id=device(0, k), device_id_type=MESH)
    expected = n_rows - 1
    for d in sorted(offsets, key=abs, reverse=True):
        present = exists(d)
        steps = (0, 1, -1) if abs(d) == 1 else (0,)
        expected = expected + jnp.where(present, len(steps), 0)

        @pl.when(present)
        def _(d=d, steps=steps):
            for k in steps:
                pl.semaphore_signal(barrier, inc=1, device_id=device(d, k), device_id_type=MESH)

    load_lens = pltpu.make_async_copy(lengths, lens, load_sem.at[1])
    load_lens.start()
    load_vecs = []
    for i, vec in enumerate((gain_one, shift_one, bias_one, gain_two, shift_two, bias_two)):
        load_vecs.append(pltpu.make_async_copy(vec, vecs.at[i], load_sem.at[2 + i]))
    load_one, load_two = [], []
    for dx in range(3):
        load_one.append(
            pltpu.make_async_copy(
                conv_one.at[:, :, dx], taps_one.at[:, :, :, pl.ds(dx * width, width)], load_sem.at[8 + dx]
            )
        )
        load_two.append(
            pltpu.make_async_copy(
                conv_two.at[:, :, dx], taps_two.at[:, :, :, pl.ds(dx * width, width)], load_sem.at[11 + dx]
            )
        )
    for load in load_vecs + load_one + load_two:
        load.start()

    class Halo:
        def __init__(self, block, half):
            own, prior = pl.ds(count, count), pl.ds(0, count)
            whole, last, head = pl.ds(1, height), pl.ds(height, 1), pl.ds(1, 1)
            above, below = pl.ds(0, 1), pl.ds(height + 1, 1)
            plans = [
                (own, last, own, above, 0, 1),
                (own, head, own, below, 0, -1),
                (own, last, prior, above, 1, 1),
                (own, head, prior, below, 1, -1),
                (own, whole, prior, whole, 1, 0),
            ]
            copies = [
                pltpu.make_async_remote_copy(
                    src_ref=block.at[f, src],
                    dst_ref=block.at[g, dst],
                    send_sem=halo_send.at[half, i],
                    recv_sem=halo_recv.at[half, i],
                    device_id=device(d, k),
                    device_id_type=MESH,
                )
                for i, (f, src, g, dst, d, k) in enumerate(plans)
            ]
            self.beside, self.onward = copies[:2], copies[2:]

        def start(self):
            for copy in self.beside:
                copy.start()

            @pl.when(exists(1))
            def _():
                for copy in self.onward:
                    copy.start()

        def wait_recv(self):
            for copy in self.beside:
                copy.wait_recv()

            @pl.when(exists(-1))
            def _():
                for copy in self.onward:
                    copy.wait_recv()

        def wait_send(self):
            for copy in self.beside:
                copy.wait_send()

            @pl.when(exists(1))
            def _():
                for copy in self.onward:
                    copy.wait_send()

    class Rows:
        def __init__(self, slots, half):
            self.copies = [
                pltpu.make_async_remote_copy(
                    src_ref=slots.at[pl.ds(0, 1)],
                    dst_ref=slots.at[pl.ds(k, 1)],
                    send_sem=row_send.at[half, k],
                    recv_sem=row_recv.at[half, k],
                    device_id=device(0, k),
                    device_id_type=MESH,
                )
                for k in range(1, n_rows)
            ]

        def start(self):
            for copy in self.copies:
                copy.start()

        def wait_recv(self):
            for copy in self.copies:
                copy.wait_recv()

        def wait_send(self):
            for copy in self.copies:
                copy.wait_send()

    class Frames:
        def __init__(self, slots, half):
            self.copies = [
                pltpu.make_async_remote_copy(
                    src_ref=slots.at[pl.ds(0, 1)],
                    dst_ref=slots.at[pl.ds(1 + i, 1)],
                    send_sem=tm_send.at[half, i],
                    recv_sem=tm_recv.at[half, i],
                    device_id=device(d, 0),
                    device_id_type=MESH,
                )
                for i, d in enumerate(offsets)
            ]

        def start(self):
            for copy, d in zip(self.copies, offsets):
                pl.when(exists(d))(copy.start)

        def wait_recv(self):
            for copy, d in zip(self.copies, offsets):
                pl.when(exists(-d))(copy.wait_recv)

        def wait_send(self):
            for copy, d in zip(self.copies, offsets):
                pl.when(exists(d))(copy.wait_send)

    members = width // GROUPS
    per_block = float(height * cols * members)
    per_frame = per_block * n_rows
    quarter = lax.rem(lax.broadcasted_iota(jnp.int32, (1, width), 1), 2 * count)

    def local_stats(block):
        packed = jnp.zeros((1, width), jnp.float32)
        for f in range(count):
            values = block[count + f, 1 : height + 1].reshape(height * cols, width).astype(jnp.float32)
            total = jnp.sum(values, axis=0, keepdims=True)
            mean = total * (members / per_block)
            off = values - mean
            squares = jnp.sum(off * off, axis=0, keepdims=True)
            total = group_total(total, members)
            off = mean - total * (1.0 / per_block)
            squares = group_total(squares + off * off * (per_block / members), members)
            packed = jnp.where(quarter == f, total, packed)
            packed = jnp.where(quarter == count + f, squares, packed)
        return packed

    def merged_rows(slots):
        parts = slots[...]
        total = jnp.sum(parts, axis=0, keepdims=True)
        off = parts * (1.0 / per_block) - total * (1.0 / per_frame)
        between = jnp.sum(off * off, axis=0, keepdims=True) * per_block
        return total + jnp.where(quarter < count, 0.0, pltpu.roll(between, count, 1))

    def merged_frames(slots, inside, length):
        parts = slots[...]
        total = jnp.sum(jnp.where(inside, parts, 0.0), axis=0, keepdims=True)
        entries = length.astype(jnp.float32) * per_frame
        mean = group_total(jnp.where(quarter < count, total, 0.0), members) / entries
        off = parts * (1.0 / per_frame) - mean
        between = jnp.sum(jnp.where(inside, off * off, 0.0), axis=0, keepdims=True) * per_frame
        var = group_total(jnp.where(quarter < count, between, total), members) / entries
        return mean, lax.rsqrt(var + 1e-6)

    def activate(block, stats, gain, shift):
        top = row == 0
        bottom = row == n_rows - 1
        for f in range(2 * count):
            mean, scale = stats[max(f - count, 0)]
            factor = scale * gain
            for i in range(height + 2):
                v = (block[f, i].astype(jnp.float32) - mean) * factor + shift
                v = v * (0.5 * jnp.tanh(0.5 * v) + 0.5)
                if i == 0:
                    v = jnp.where(top, 0.0, v)
                if i == height + 1:
                    v = jnp.where(bottom, 0.0, v)
                act[f, i] = v.astype(jnp.bfloat16)

    def conv(taps, sources):
        lefts = []
        for f in range(count):
            pieces = []
            for dt in range(3):
                for dy in range(3):
                    pieces.append(
                        act[sources[f][dt], dy : dy + height].reshape(height * cols, width)
                    )
            lefts.append(jnp.concatenate(pieces, axis=1))
        left = jnp.concatenate(lefts, axis=0)
        right = taps[...].reshape(9 * width, 3 * width)
        return jnp.dot(left, right, preferred_element_type=jnp.float32)

    column = lax.broadcasted_iota(jnp.int32, (cols, width), 0)

    def joined(wide, i):
        y = wide[i * cols : (i + 1) * cols]
        before = pltpu.roll(y[:, :width], 1, 0)
        after = pltpu.roll(y[:, 2 * width :], cols - 1, 0)
        return (
            y[:, width : 2 * width]
            + jnp.where(column == 0, 0.0, before)
            + jnp.where(column == cols - 1, 0.0, after)
        )

    load_frames.wait()
    rows_one[pl.ds(0, 1)] = local_stats(raw)
    pl.semaphore_wait(barrier, expected)
    row_sums = Rows(rows_one, 0)
    row_sums.start()
    halo_one = Halo(raw, 0)
    halo_one.start()

    load_lens.wait()
    starts, stops = [], []
    for f in range(count):
        start = jnp.int32(0)
        stop = jnp.int32(0)
        offset = jnp.int32(0)
        for v in range(videos):
            size = lens[v]
            here = offset <= first + f
            start = jnp.where(here, offset, start)
            stop = jnp.where(here, offset + size, stop)
            offset = offset + size
        starts.append(start)
        stops.append(stop)
    slot = lax.broadcasted_iota(jnp.int32, tms_one.shape, 0)
    lane = lax.broadcasted_iota(jnp.int32, tms_one.shape, 1)
    far = (slot + 1) // 2
    home = tm - jnp.where(lax.rem(slot, 2) == 1, far, -far)
    frame = home * count + lax.rem(lane, count)
    known = slot <= len(offsets)
    inside = [known & (frame >= starts[f]) & (frame < stops[f]) for f in range(count)]
    sources = [
        [jnp.maximum(f + dt, starts[f] - first + 2) for dt in range(3)] for f in range(count)
    ]

    row_sums.wait_recv()
    tms_one[pl.ds(0, 1)] = merged_rows(rows_one)
    tm_sums = Frames(tms_one, 0)
    tm_sums.start()
    for load in load_vecs:
        load.wait()
    tm_sums.wait_recv()
    stats = [merged_frames(tms_one, inside[f], stops[f] - starts[f]) for f in range(count)]
    halo_one.wait_recv()
    activate(raw, stats, vecs[0:1], vecs[1:2])
    for load in load_one:
        load.wait()
    wide = conv(taps_one, sources)
    for f in range(count):
        for i in range(height):
            mid[count + f, 1 + i] = (joined(wide, f * height + i) + vecs[2:3]).astype(jnp.bfloat16)
    row_sums.wait_send()
    tm_sums.wait_send()
    halo_one.wait_send()

    rows_two[pl.ds(0, 1)] = local_stats(mid)
    row_sums = Rows(rows_two, 1)
    row_sums.start()
    halo_two = Halo(mid, 1)
    halo_two.start()
    row_sums.wait_recv()
    tms_two[pl.ds(0, 1)] = merged_rows(rows_two)
    tm_sums = Frames(tms_two, 1)
    tm_sums.start()
    tm_sums.wait_recv()
    stats = [merged_frames(tms_two, inside[f], stops[f] - starts[f]) for f in range(count)]
    halo_two.wait_recv()
    activate(mid, stats, vecs[3:4], vecs[4:5])
    for load in load_two:
        load.wait()
    wide = conv(taps_two, sources)
    for f in range(count):
        for i in range(height):
            out[f, i] = (
                joined(wide, f * height + i) + vecs[5:6] + raw[count + f, 1 + i].astype(jnp.float32)
            )
    row_sums.wait_send()
    tm_sums.wait_send()
    halo_two.wait_send()


def per_device(n_tm, n_rows, *args):
    frames, lengths = args[0], args[1]
    count, height, cols, width = frames.shape
    near = len(tm_offsets(n_tm, count))
    window = -(-(1 + near) // 8) * 8
    block = pltpu.VMEM((2 * count, height + 2, cols, width), jnp.bfloat16)
    taps = pltpu.VMEM((3, 3, width, 3 * width), jnp.bfloat16)
    return pl.pallas_call(
        functools.partial(kernel, n_tm, n_rows),
        out_shape=pltpu.VMEM(frames.shape, jnp.float32),
        in_specs=[pl.BlockSpec(memory_space=pl.ANY)] * len(args),
        out_specs=pl.BlockSpec(memory_space=pltpu.VMEM),
        scratch_shapes=[
            block, block, block, taps, taps,
            pltpu.VMEM((8, width), jnp.float32),
            pltpu.SMEM(lengths.shape, jnp.int32),
            pltpu.VMEM((n_rows, width), jnp.float32),
            pltpu.VMEM((n_rows, width), jnp.float32),
            pltpu.VMEM((window, width), jnp.float32),
            pltpu.VMEM((window, width), jnp.float32),
            pltpu.SemaphoreType.DMA((14,)),
            pltpu.SemaphoreType.DMA((2, 5)),
            pltpu.SemaphoreType.DMA((2, 5)),
            pltpu.SemaphoreType.DMA((2, n_rows)),
            pltpu.SemaphoreType.DMA((2, n_rows)),
            pltpu.SemaphoreType.DMA((2, near)),
            pltpu.SemaphoreType.DMA((2, near)),
        ],
        compiler_params=pltpu.CompilerParams(
            collective_id=0, has_side_effects=True, vmem_limit_bytes=40 * 1024 * 1024
        ),
        name="residual_block",
    )(*[pltpu.with_memory_space_constraint(a, pltpu.HBM) for a in args])


def solution(mesh):
    placed = (P("tm", "rows", None, None), P(), P(), P(), P(), P(), P(), P(), P(), P())
    return jax.shard_map(
        functools.partial(per_device, mesh.shape["tm"], mesh.shape["rows"]),
        mesh=mesh,
        in_specs=placed,
        out_specs=P("tm", "rows", None, None),
        check_vma=False,
    )
```

```python
import functools

import jax
import jax.numpy as jnp
from jax import lax
from jax.experimental import pallas as pl
from jax.experimental.pallas import tpu as pltpu
from jax.sharding import PartitionSpec as P

GROUPS = 32
MOST = 16
MESH = pl.DeviceIdType.MESH


def tm_offsets(n_tm, count):
    reach = min(-(-(MOST - 1) // count), n_tm - 1)
    return [d for far in range(1, reach + 1) for d in (far, -far)]


def tm_hops(d):
    return abs(d) // 4 + min(abs(d) % 4, 4 - abs(d) % 4)


def wrapped(index, offset, size):
    return lax.rem(index + (offset + size), size)


def neighbours(row):
    lanes = row.shape[1]
    return {s: pltpu.roll(row, s % lanes, 1) if s else row for s in range(-3, 4)}


def by_place(place, choices):
    picked = choices[-1]
    for i in range(len(choices) - 1):
        picked = jnp.where(place == i, choices[i], picked)
    return picked


def group_total(row, place):
    near = neighbours(row)
    sums = [near[i] + near[i - 1] + (near[i - 2] + near[i - 3]) for i in range(4)]
    return by_place(place, sums)


def await_signals(semaphore, number):
    @pl.when(number > 0)
    def _():
        pl.semaphore_wait(semaphore, number)


def kernel(
    n_tm, n_rows,
    frames, lengths, gain_one, shift_one, conv_one, bias_one, gain_two, shift_two, conv_two, bias_two,
    out,
    raw, mid, act, taps_one, taps_two, vecs, lens, rows_one, rows_two, tms_one, tms_two,
    ready, load_sem, halo_send, halo_recv, row_send, row_recv, tm_send, tm_recv,
):
    count, height, cols, width = frames.shape
    videos = lengths.shape[0]
    tm = lax.axis_index("tm")
    row = lax.axis_index("rows")
    first = tm * count
    offsets = tm_offsets(n_tm, count)

    load_frames = pltpu.make_async_copy(
        frames, raw.at[pl.ds(count, count), pl.ds(1, height)], load_sem.at[0]
    )
    load_frames.start()

    def exists(d):
        return (tm + d >= 0) & (tm + d < n_tm)

    def device(d, k):
        return {"tm": tm + d, "rows": wrapped(row, k, n_rows)}

    host = n_rows > 1 and 1
    hosting = row == host
    reach = max(offsets)
    below = jnp.minimum(tm, reach)
    above = jnp.minimum(n_tm - 1 - tm, reach)
    barrier = pltpu.get_barrier_semaphore()
    full, answers, complete = ready.at[0], ready.at[1], ready.at[2]

    def signal(semaphore, target):
        pl.semaphore_signal(semaphore, inc=1, device_id=target, device_id_type=MESH)

    def tell_rows(semaphore):
        @pl.when(hosting)
        def _():
            for k in sorted(range(1, n_rows), key=lambda k: -min(k, n_rows - k)):
                signal(semaphore, device(0, k))

    tell_rows(barrier)
    for d in range(reach, 0, -1):

        @pl.when(exists(d))
        def _(d=d):
            signal(barrier, device(d, 0))

    announced = below + jnp.where(hosting, 0, 1)

    def answer():
        for d in range(1, reach + 1):

            @pl.when(exists(-d))
            def _(d=d):
                signal(ready.at[2 + d], device(-d, 0))

        @pl.when(jnp.logical_not(hosting))
        def _():
            signal(answers, {"tm": tm, "rows": host})

    load_lens = pltpu.make_async_copy(lengths, lens, load_sem.at[1])
    load_lens.start()
    for i, vec in enumerate((gain_one, shift_one, bias_one, gain_two, shift_two, bias_two)):
        pltpu.make_async_copy(vec, vecs.at[i], load_sem.at[2]).start()
    for dx in range(3):
        for i, (source, held) in enumerate(((conv_one, taps_one), (conv_two, taps_two))):
            pltpu.make_async_copy(
                source.at[:, :, dx], held.at[:, :, :, pl.ds(dx * width, width)], load_sem.at[3 + i]
            ).start()
    load_vecs = pltpu.make_async_copy(vecs.at[pl.ds(0, 6)], vecs.at[pl.ds(0, 6)], load_sem.at[2])
    load_one = pltpu.make_async_copy(taps_one, taps_one, load_sem.at[3])
    load_two = pltpu.make_async_copy(taps_two, taps_two, load_sem.at[4])

    def remote(src, dst, send, recv, d, k):
        return pltpu.make_async_remote_copy(
            src_ref=src,
            dst_ref=dst,
            send_sem=send,
            recv_sem=recv,
            device_id=device(d, k),
            device_id_type=MESH,
        )

    class Halo:
        def __init__(self, block, half):
            own, prior = pl.ds(count, count), pl.ds(0, count)
            whole, last, head = pl.ds(1, height), pl.ds(height, 1), pl.ds(1, 1)
            above, below = pl.ds(0, 1), pl.ds(height + 1, 1)

            def copy(f, src, g, dst, d, k):
                sems = halo_send.at[half, d], halo_recv.at[half, d]
                return remote(block.at[f, src], block.at[g, dst], *sems, d, k)

            self.beside = [copy(own, last, own, above, 0, 1), copy(own, head, own, below, 0, -1)]
            self.onward = copy(own, whole, prior, whole, 1, 0)
            self.corners = [copy(own, last, prior, above, 1, 1), copy(own, head, prior, below, 1, -1)]
            edge = block.at[:, pl.ds(0, 1)]
            self.all_beside = remote(edge, edge, halo_send.at[half, 0], halo_recv.at[half, 0], 0, 1)
            front = block.at[prior]
            self.all_onward = remote(front, front, halo_send.at[half, 1], halo_recv.at[half, 1], 0, 1)

        def start_beside(self):
            for copy in self.beside:
                copy.start()

        def start_onward(self):
            pl.when(exists(1))(self.onward.start)

        def start_corners(self):
            @pl.when(exists(1))
            def _():
                for copy in self.corners:
                    copy.start()

        def wait_recv(self):
            self.all_beside.wait_recv()
            pl.when(exists(-1))(self.all_onward.wait_recv)

        def wait_send(self):
            self.all_beside.wait_send()
            pl.when(exists(1))(self.all_onward.wait_send)

    class Rows:
        def __init__(self, slots, half):
            sems = row_send.at[half], row_recv.at[half]
            self.copies = [
                remote(slots.at[pl.ds(0, 1)], slots.at[pl.ds(k, 1)], *sems, 0, k) for k in range(1, n_rows)
            ]
            others = slots.at[pl.ds(1, n_rows - 1)]
            self.all = remote(others, others, *sems, 0, 1)

        def start(self):
            for k in sorted(range(1, n_rows), key=lambda k: -min(k, n_rows - k)):
                self.copies[k - 1].start()

    class Frames:
        def __init__(self, slots, half):
            sems = tm_send.at[half], tm_recv.at[half]
            self.copies = {
                d: remote(slots.at[pl.ds(0, 1)], slots.at[pl.ds(1 + i, 1)], *sems, d, 0)
                for i, d in enumerate(offsets)
            }
            self.all = {}
            for n in range(reach, 2 * reach + 1):
                others = slots.at[pl.ds(1, n)]
                self.all[n] = remote(others, others, *sems, 0, 1)

        def start(self, *signs):
            for d in sorted(range(1, reach + 1), key=lambda d: -tm_hops(d)):
                for sign in signs:
                    pl.when(exists(sign * d))(self.copies[sign * d].start)

        def wait_recv(self):
            for n in self.all:
                pl.when(below + above == n)(self.all[n].wait_recv)

        def wait_send(self):
            for n in self.all:
                pl.when(below + above == n)(self.all[n].wait_send)

    members = width // GROUPS
    per_block = float(height * cols * members)
    place = lax.rem(lax.broadcasted_iota(jnp.int32, (1, width), 1), members)
    odd = lax.rem(place, 2) == 1
    head = place < 2

    def local_stats(block):
        totals, squares = [], []
        for f in range(count):
            values = block[count + f, 1 : height + 1].reshape(height * cols, width).astype(jnp.float32)
            total = jnp.sum(values, axis=0, keepdims=True)
            mean = total * (members / per_block)
            off = values - mean
            square = jnp.sum(off * off, axis=0, keepdims=True)
            total = group_total(total, place)
            off = mean - total * (1.0 / per_block)
            totals.append(total)
            squares.append(group_total(square + off * off * (per_block / members), place))
        return by_place(place, totals + squares)

    def video_sums(slots, inside, entries):
        parts = slots[...]
        merged = []
        for f in range(count):
            total = jnp.sum(jnp.where(inside[f], parts, 0.0), axis=0, keepdims=True)
            total = total + jnp.where(odd, pltpu.roll(total, 1, 1), pltpu.roll(total, width - 1, 1))
            off = parts * (1.0 / per_block) - total * (1.0 / entries[f])
            between = jnp.sum(jnp.where(inside[f], off * off, 0.0), axis=0, keepdims=True) * per_block
            between = pltpu.roll(between, 2, 1) + jnp.where(
                odd, pltpu.roll(between, 3, 1), pltpu.roll(between, 1, 1)
            )
            merged.append(total + jnp.where(head, 0.0, between))
        return jnp.where(odd, merged[1], merged[0])

    def video_stats(slots, entries):
        parts = slots[...]
        share = jnp.where(odd, entries[1], entries[0])
        total = jnp.sum(parts, axis=0, keepdims=True)
        mean = total / (share * n_rows)
        off = parts * (1.0 / share) - mean
        between = jnp.sum(off * off, axis=0, keepdims=True) * share
        var = (total + pltpu.roll(between, 2, 1)) / (share * n_rows)
        near = neighbours(jnp.where(head, mean, lax.rsqrt(var + 1e-6)))
        spread = [by_place(place, [near[i - k] for i in range(4)]) for k in range(4)]
        return [(spread[f], spread[count + f]) for f in range(count)]

    def activate(block, stats, gain, shift):
        top = row == 0
        bottom = row == n_rows - 1
        for f in range(2 * count):
            mean, scale = stats[max(f - count, 0)]
            factor = scale * gain
            for i in range(height + 2):
                v = (block[f, i].astype(jnp.float32) - mean) * factor + shift
                v = v * (0.5 * jnp.tanh(0.5 * v) + 0.5)
                if i == 0:
                    v = jnp.where(top, 0.0, v)
                if i == height + 1:
                    v = jnp.where(bottom, 0.0, v)
                act[f, i] = v.astype(jnp.bfloat16)

    def conv(taps, sources):
        lefts = []
        for f in range(count):
            pieces = []
            for dt in range(3):
                for dy in range(3):
                    pieces.append(
                        act[sources[f][dt], dy : dy + height].reshape(height * cols, width)
                    )
            lefts.append(jnp.concatenate(pieces, axis=1))
        left = jnp.concatenate(lefts, axis=0)
        right = taps[...].reshape(9 * width, 3 * width)
        return jnp.dot(left, right, preferred_element_type=jnp.float32)

    column = lax.broadcasted_iota(jnp.int32, (cols, width), 0)

    def joined(wide, i):
        y = wide[i * cols : (i + 1) * cols]
        before = pltpu.roll(y[:, :width], 1, 0)
        after = pltpu.roll(y[:, 2 * width :], cols - 1, 0)
        return (
            y[:, width : 2 * width]
            + jnp.where(column == 0, 0.0, before)
            + jnp.where(column == cols - 1, 0.0, after)
        )

    load_frames.wait()
    tms_one[pl.ds(0, 1)] = local_stats(raw)
    await_signals(barrier, announced)
    tm_sums = Frames(tms_one, 0)
    tm_sums.start(-1)
    answer()

    load_lens.wait()
    starts, stops = [], []
    for f in range(count):
        start = jnp.int32(0)
        stop = jnp.int32(0)
        offset = jnp.int32(0)
        for v in range(videos):
            size = lens[v]
            here = offset <= first + f
            start = jnp.where(here, offset, start)
            stop = jnp.where(here, offset + size, stop)
            offset = offset + size
        starts.append(start)
        stops.append(stop)
    entries = [(stops[f] - starts[f]).astype(jnp.float32) * per_block for f in range(count)]
    slot = lax.broadcasted_iota(jnp.int32, tms_one.shape, 0)
    lane = lax.broadcasted_iota(jnp.int32, tms_one.shape, 1)
    far = (slot + 1) // 2
    home = tm - jnp.where(lax.rem(slot, 2) == 1, far, -far)
    frame = home * count + lax.rem(lane, count)
    known = slot <= len(offsets)
    inside = [known & (frame >= starts[f]) & (frame < stops[f]) for f in range(count)]
    sources = [
        [jnp.maximum(f + dt, starts[f] - first + 2) for dt in range(3)] for f in range(count)
    ]

    for d in range(1, reach + 1):

        @pl.when(exists(d))
        def _(d=d):
            pl.semaphore_wait(ready.at[2 + d], 1)
            tm_sums.copies[d].start()

    halo_one = Halo(raw, 0)
    halo_one.start_onward()

    @pl.when(hosting)
    def _():
        pl.semaphore_wait(answers, n_rows - 1)

    tell_rows(complete)

    @pl.when(jnp.logical_not(hosting))
    def _():
        pl.semaphore_wait(complete, 1)

    @pl.when(exists(-1))
    def _():
        signal(full, device(-1, 0))

    tm_sums.wait_recv()
    rows_one[pl.ds(0, 1)] = video_sums(tms_one, inside, entries)
    row_sums = Rows(rows_one, 0)
    row_sums.start()
    halo_one.start_beside()

    @pl.when(exists(1))
    def _():
        pl.semaphore_wait(full, 1)

    halo_one.start_corners()
    load_vecs.wait()
    row_sums.all.wait_recv()
    stats = video_stats(rows_one, entries)
    halo_one.wait_recv()
    activate(raw, stats, vecs[0:1], vecs[1:2])
    load_one.wait()
    wide = conv(taps_one, sources)
    for f in range(count):
        for i in range(height):
            mid[count + f, 1 + i] = (joined(wide, f * height + i) + vecs[2:3]).astype(jnp.bfloat16)
    tm_sums.wait_send()
    row_sums.all.wait_send()
    halo_one.wait_send()

    tms_two[pl.ds(0, 1)] = local_stats(mid)
    tm_sums = Frames(tms_two, 1)
    tm_sums.start(-1, 1)
    halo_two = Halo(mid, 1)
    halo_two.start_beside()
    halo_two.start_corners()
    halo_two.start_onward()
    tm_sums.wait_recv()
    rows_two[pl.ds(0, 1)] = video_sums(tms_two, inside, entries)
    row_sums = Rows(rows_two, 1)
    row_sums.start()
    row_sums.all.wait_recv()
    stats = video_stats(rows_two, entries)
    halo_two.wait_recv()
    activate(mid, stats, vecs[3:4], vecs[4:5])
    load_two.wait()
    wide = conv(taps_two, sources)
    for f in range(count):
        for i in range(height):
            out[f, i] = (
                joined(wide, f * height + i) + vecs[5:6] + raw[count + f, 1 + i].astype(jnp.float32)
            )
    tm_sums.wait_send()
    row_sums.all.wait_send()
    halo_two.wait_send()


def per_device(n_tm, n_rows, *args):
    frames, lengths = args[0], args[1]
    count, height, cols, width = frames.shape
    near = len(tm_offsets(n_tm, count))
    window = -(-(1 + near) // 8) * 8
    block = pltpu.VMEM((2 * count, height + 2, cols, width), jnp.bfloat16)
    taps = pltpu.VMEM((3, 3, width, 3 * width), jnp.bfloat16)
    return pl.pallas_call(
        functools.partial(kernel, n_tm, n_rows),
        out_shape=pltpu.VMEM(frames.shape, jnp.float32),
        in_specs=[pl.BlockSpec(memory_space=pl.ANY)] * len(args),
        out_specs=pl.BlockSpec(memory_space=pltpu.VMEM),
        scratch_shapes=[
            block, block, block, taps, taps,
            pltpu.VMEM((8, width), jnp.float32),
            pltpu.SMEM(lengths.shape, jnp.int32),
            pltpu.VMEM((n_rows, width), jnp.float32),
            pltpu.VMEM((n_rows, width), jnp.float32),
            pltpu.VMEM((window, width), jnp.float32),
            pltpu.VMEM((window, width), jnp.float32),
            pltpu.SemaphoreType.REGULAR((3 + near // 2 + 1,)),
            pltpu.SemaphoreType.DMA((5,)),
            pltpu.SemaphoreType.DMA((2, 2)),
            pltpu.SemaphoreType.DMA((2, 2)),
            pltpu.SemaphoreType.DMA((2,)),
            pltpu.SemaphoreType.DMA((2,)),
            pltpu.SemaphoreType.DMA((2,)),
            pltpu.SemaphoreType.DMA((2,)),
        ],
        compiler_params=pltpu.CompilerParams(
            collective_id=0, has_side_effects=True, vmem_limit_bytes=40 * 1024 * 1024
        ),
        name="residual_block",
    )(*[pltpu.with_memory_space_constraint(a, pltpu.HBM) for a in args])


def solution(mesh):
    placed = (P("tm", "rows", None, None), P(), P(), P(), P(), P(), P(), P(), P(), P())
    return jax.shard_map(
        functools.partial(per_device, mesh.shape["tm"], mesh.shape["rows"]),
        mesh=mesh,
        in_specs=placed,
        out_specs=P("tm", "rows", None, None),
        check_vma=False,
    )
```

```python
import functools

import jax
import jax.numpy as jnp
from jax import lax
from jax.experimental import pallas as pl
from jax.experimental.pallas import tpu as pltpu
from jax.sharding import PartitionSpec as P

GROUPS = 32
MOST = 16
MESH = pl.DeviceIdType.MESH


def tm_offsets(n_tm, count):
    reach = min(-(-(MOST - 1) // count), n_tm - 1)
    return [d for far in range(1, reach + 1) for d in (far, -far)]


def tm_hops(d):
    return abs(d) // 4 + min(abs(d) % 4, 4 - abs(d) % 4)


def wrapped(index, offset, size):
    return lax.rem(index + (offset + size), size)


def neighbours(row):
    lanes = row.shape[1]
    return {s: pltpu.roll(row, s % lanes, 1) if s else row for s in range(-3, 4)}


def by_place(place, choices):
    picked = choices[-1]
    for i in range(len(choices) - 1):
        picked = jnp.where(place == i, choices[i], picked)
    return picked


def group_total(row, place):
    near = neighbours(row)
    sums = [near[i] + near[i - 1] + (near[i - 2] + near[i - 3]) for i in range(4)]
    return by_place(place, sums)


def await_signals(semaphore, number):
    @pl.when(number > 0)
    def _():
        pl.semaphore_wait(semaphore, number)


def kernel(
    n_tm, n_rows,
    frames, lengths, gain_one, shift_one, conv_one, bias_one, gain_two, shift_two, conv_two, bias_two,
    out,
    raw, mid, taps_one, taps_two, vecs, lens, rows_one, rows_two, tms_one, tms_two,
    ready, load_sem, halo_send, halo_recv, row_send, row_recv, tm_send, tm_recv,
):
    count, height, cols, width = frames.shape
    videos = lengths.shape[0]
    tm = lax.axis_index("tm")
    row = lax.axis_index("rows")
    first = tm * count
    offsets = tm_offsets(n_tm, count)

    load_frames = pltpu.make_async_copy(
        frames, raw.at[pl.ds(count, count), pl.ds(1, height)], load_sem.at[0]
    )
    load_frames.start()

    def exists(d):
        return (tm + d >= 0) & (tm + d < n_tm)

    def device(d, k):
        return {"tm": tm + d, "rows": wrapped(row, k, n_rows)}

    host = n_rows > 1 and 1
    hosting = row == host
    reach = max(offsets)
    below = jnp.minimum(tm, reach)
    above = jnp.minimum(n_tm - 1 - tm, reach)
    barrier = pltpu.get_barrier_semaphore()
    full, answers, complete = ready.at[0], ready.at[1], ready.at[2]

    def signal(semaphore, target):
        pl.semaphore_signal(semaphore, inc=1, device_id=target, device_id_type=MESH)

    def tell_rows(semaphore):
        @pl.when(hosting)
        def _():
            for k in sorted(range(1, n_rows), key=lambda k: -min(k, n_rows - k)):
                signal(semaphore, device(0, k))

    for d in range(1, reach + 1):

        @pl.when(exists(d))
        def _(d=d):
            signal(barrier, device(d, 0))

    tell_rows(barrier)
    announced = below + jnp.where(hosting, 0, 1)

    def answer():
        for d in range(1, reach + 1):

            @pl.when(exists(-d))
            def _(d=d):
                signal(ready.at[2 + d], device(-d, 0))

        @pl.when(jnp.logical_not(hosting))
        def _():
            signal(answers, {"tm": tm, "rows": host})

    load_lens = pltpu.make_async_copy(lengths, lens, load_sem.at[1])
    load_lens.start()
    for i, vec in enumerate((gain_one, shift_one, bias_one, gain_two, shift_two, bias_two)):
        pltpu.make_async_copy(vec, vecs.at[i], load_sem.at[2]).start()
    for dx in range(3):
        for i, (source, held) in enumerate(((conv_one, taps_one), (conv_two, taps_two))):
            pltpu.make_async_copy(
                source.at[:, :, dx], held.at[:, :, :, pl.ds(dx * width, width)], load_sem.at[3 + i]
            ).start()
    load_vecs = pltpu.make_async_copy(vecs.at[pl.ds(0, 6)], vecs.at[pl.ds(0, 6)], load_sem.at[2])
    load_one = pltpu.make_async_copy(taps_one, taps_one, load_sem.at[3])
    load_two = pltpu.make_async_copy(taps_two, taps_two, load_sem.at[4])

    def remote(src, dst, send, recv, d, k):
        return pltpu.make_async_remote_copy(
            src_ref=src,
            dst_ref=dst,
            send_sem=send,
            recv_sem=recv,
            device_id=device(d, k),
            device_id_type=MESH,
        )

    class Halo:
        def __init__(self, block, half):
            own, prior = pl.ds(count, count), pl.ds(0, count)
            whole, last, head = pl.ds(1, height), pl.ds(height, 1), pl.ds(1, 1)
            above, below = pl.ds(0, 1), pl.ds(height + 1, 1)

            def copy(f, src, g, dst, d, k):
                sems = halo_send.at[half, d], halo_recv.at[half, d]
                return remote(block.at[f, src], block.at[g, dst], *sems, d, k)

            self.beside = [copy(own, last, own, above, 0, 1), copy(own, head, own, below, 0, -1)]
            halves = [(pl.ds(count + f, 1), pl.ds(f, 1)) for f in range(count)]
            self.onward = [copy(src, whole, dst, whole, 1, 0) for src, dst in halves]
            self.corners = [copy(own, last, prior, above, 1, 1), copy(own, head, prior, below, 1, -1)]
            edge = block.at[:, pl.ds(0, 1)]
            self.all_beside = remote(edge, edge, halo_send.at[half, 0], halo_recv.at[half, 0], 0, 1)
            front = block.at[prior]
            self.all_onward = remote(front, front, halo_send.at[half, 1], halo_recv.at[half, 1], 0, 1)

        def start_beside(self):
            for copy in self.beside:
                copy.start()

        def start_onward(self, *halves):
            @pl.when(exists(1))
            def _():
                for half in halves:
                    self.onward[half].start()

        def start_corners(self):
            @pl.when(exists(1))
            def _():
                for copy in self.corners:
                    copy.start()

        def wait_recv(self):
            self.all_beside.wait_recv()
            pl.when(exists(-1))(self.all_onward.wait_recv)

        def wait_send(self):
            self.all_beside.wait_send()
            pl.when(exists(1))(self.all_onward.wait_send)

    class Rows:
        def __init__(self, slots, half):
            sems = row_send.at[half], row_recv.at[half]
            self.copies = [
                remote(slots.at[pl.ds(0, 1)], slots.at[pl.ds(k, 1)], *sems, 0, k) for k in range(1, n_rows)
            ]
            others = slots.at[pl.ds(1, n_rows - 1)]
            self.all = remote(others, others, *sems, 0, 1)

        def start(self):
            for k in sorted(range(1, n_rows), key=lambda k: -min(k, n_rows - k)):
                self.copies[k - 1].start()

    class Frames:
        def __init__(self, slots, half):
            sems = tm_send.at[half], tm_recv.at[half]
            self.copies = {
                d: remote(slots.at[pl.ds(0, 1)], slots.at[pl.ds(1 + i, 1)], *sems, d, 0)
                for i, d in enumerate(offsets)
            }
            self.all = {}
            for n in range(reach, 2 * reach + 1):
                others = slots.at[pl.ds(1, n)]
                self.all[n] = remote(others, others, *sems, 0, 1)

        def start(self, *signs):
            for d in sorted(range(1, reach + 1), key=lambda d: -tm_hops(d)):
                for sign in signs:
                    pl.when(exists(sign * d))(self.copies[sign * d].start)

        def wait_recv(self):
            for n in self.all:
                pl.when(below + above == n)(self.all[n].wait_recv)

        def wait_send(self):
            for n in self.all:
                pl.when(below + above == n)(self.all[n].wait_send)

    members = width // GROUPS
    per_block = float(height * cols * members)
    place = lax.rem(lax.broadcasted_iota(jnp.int32, (1, width), 1), members)
    odd = lax.rem(place, 2) == 1
    head = place < 2

    def local_stats(frames_rows):
        totals, squares = [], []
        for rows in frames_rows:
            near = jnp.sum(rows[0].astype(jnp.float32), axis=0, keepdims=True) * (1.0 / cols)
            first_sum = jnp.zeros((cols, width), jnp.float32)
            second_sum = jnp.zeros((cols, width), jnp.float32)
            for values in rows:
                off = values.astype(jnp.float32) - near
                first_sum = first_sum + off
                second_sum = second_sum + off * off
            first_sum = jnp.sum(first_sum, axis=0, keepdims=True)
            second_sum = jnp.sum(second_sum, axis=0, keepdims=True)
            shift = first_sum * (1.0 / (height * cols))
            total = group_total(first_sum + near * float(height * cols), place)
            off = near + shift - total * (1.0 / per_block)
            square = second_sum - first_sum * shift + off * off * float(height * cols)
            totals.append(total)
            squares.append(group_total(square, place))
        return by_place(place, totals + squares)

    def video_sums(slots, inside, entries):
        parts = slots[...]
        merged = []
        for f in range(count):
            total = jnp.sum(jnp.where(inside[f], parts, 0.0), axis=0, keepdims=True)
            total = total + jnp.where(odd, pltpu.roll(total, 1, 1), pltpu.roll(total, width - 1, 1))
            off = parts * (1.0 / per_block) - total * (1.0 / entries[f])
            between = jnp.sum(jnp.where(inside[f], off * off, 0.0), axis=0, keepdims=True) * per_block
            between = pltpu.roll(between, 2, 1) + jnp.where(
                odd, pltpu.roll(between, 3, 1), pltpu.roll(between, 1, 1)
            )
            merged.append(total + jnp.where(head, 0.0, between))
        return jnp.where(odd, merged[1], merged[0])

    def video_stats(slots, entries):
        parts = slots[...]
        share = jnp.where(odd, entries[1], entries[0])
        total = jnp.sum(parts, axis=0, keepdims=True)
        mean = total / (share * n_rows)
        off = parts * (1.0 / share) - mean
        between = jnp.sum(off * off, axis=0, keepdims=True) * share
        var = (total + pltpu.roll(between, 2, 1)) / (share * n_rows)
        near = neighbours(jnp.where(head, mean, lax.rsqrt(var + 1e-6)))
        spread = [by_place(place, [near[i - k] for i in range(4)]) for k in range(4)]
        return [(spread[f], spread[count + f]) for f in range(count)]

    column = lax.broadcasted_iota(jnp.int32, (cols, width), 0)

    def convolved(block, stats, gain, shift, taps):
        def active(f, i):
            mean, scale = stats[max(f - count, 0)]
            v = (block[f, i].astype(jnp.float32) - mean) * (scale * gain) + shift
            v = v * (0.5 * jnp.tanh(0.5 * v) + 0.5)
            if i == 0:
                v = jnp.where(row == 0, 0.0, v)
            if i == height + 1:
                v = jnp.where(row == n_rows - 1, 0.0, v)
            return v.astype(jnp.bfloat16)

        seen = [[[], [], []] for _ in range(count)]
        for i in range(height + 2):
            a, b, c, d = [active(f, i) for f in range(2 * count)]
            b = jnp.where(starts[0] < first, b, c)
            seen[0][0].append(jnp.where(starts[0] < first - 1, a, b))
            seen[0][1].append(b)
            seen[0][2].append(c)
            seen[1][0].append(jnp.where(starts[1] > first, d, b))
            seen[1][1].append(jnp.where(starts[1] > first, d, c))
            seen[1][2].append(d)
        right = taps[...].reshape(9 * width, 3 * width)
        results = []
        for f in range(count):
            pieces = [
                jnp.concatenate(seen[f][dt][dy : dy + height], axis=0) for dt in range(3) for dy in range(3)
            ]
            wide = jnp.dot(jnp.concatenate(pieces, axis=1), right, preferred_element_type=jnp.float32)
            rows = []
            for i in range(height):
                y = wide[i * cols : (i + 1) * cols]
                before = pltpu.roll(y[:, :width], 1, 0)
                after = pltpu.roll(y[:, 2 * width :], cols - 1, 0)
                rows.append(
                    y[:, width : 2 * width]
                    + jnp.where(column == 0, 0.0, before)
                    + jnp.where(column == cols - 1, 0.0, after)
                )
            results.append(rows)
        return results

    def frame_sums(slots):
        parts = slots[...]
        total = jnp.sum(parts, axis=0, keepdims=True)
        off = parts * (1.0 / per_block) - total * (1.0 / (per_block * n_rows))
        between = jnp.sum(off * off, axis=0, keepdims=True) * per_block
        return total + jnp.where(head, 0.0, pltpu.roll(between, 2, 1))

    def frame_stats(slots, inside, entries):
        parts = slots[...]
        per_frame = per_block * n_rows
        stats = []
        for f in range(count):
            total = jnp.sum(jnp.where(inside[f], parts, 0.0), axis=0, keepdims=True)
            mean = group_total(jnp.where(head, total, 0.0), place) / (entries[f] * n_rows)
            off = parts * (1.0 / per_frame) - mean
            between = jnp.sum(jnp.where(inside[f], off * off, 0.0), axis=0, keepdims=True) * per_frame
            var = group_total(jnp.where(head, between, total), place) / (entries[f] * n_rows)
            stats.append((mean, lax.rsqrt(var + 1e-6)))
        return stats

    load_frames.wait()
    tms_one[pl.ds(0, 1)] = local_stats(
        [[raw[count + f, 1 + i] for i in range(height)] for f in range(count)]
    )
    await_signals(barrier, announced)
    tm_sums = Frames(tms_one, 0)
    tm_sums.start(-1)
    answer()

    load_lens.wait()
    starts, stops = [], []
    for f in range(count):
        start = jnp.int32(0)
        stop = jnp.int32(0)
        offset = jnp.int32(0)
        for v in range(videos):
            size = lens[v]
            here = offset <= first + f
            start = jnp.where(here, offset, start)
            stop = jnp.where(here, offset + size, stop)
            offset = offset + size
        starts.append(start)
        stops.append(stop)
    entries = [(stops[f] - starts[f]).astype(jnp.float32) * per_block for f in range(count)]
    slot = lax.broadcasted_iota(jnp.int32, tms_one.shape, 0)
    lane = lax.broadcasted_iota(jnp.int32, tms_one.shape, 1)
    far = (slot + 1) // 2
    home = tm - jnp.where(lax.rem(slot, 2) == 1, far, -far)
    frame = home * count + lax.rem(lane, count)
    known = slot <= len(offsets)
    inside = [known & (frame >= starts[f]) & (frame < stops[f]) for f in range(count)]

    halo_one = Halo(raw, 0)
    for d in range(1, reach + 1):

        @pl.when(exists(d))
        def _(d=d):
            pl.semaphore_wait(ready.at[2 + d], 1)
            tm_sums.copies[d].start()

        if d == reach // 2:
            halo_one.start_onward(0)

    halo_one.start_onward(1)

    @pl.when(hosting)
    def _():
        pl.semaphore_wait(answers, n_rows - 1)

    tell_rows(complete)

    @pl.when(jnp.logical_not(hosting))
    def _():
        pl.semaphore_wait(complete, 1)

    @pl.when(exists(-1))
    def _():
        signal(full, device(-1, 0))

    tm_sums.wait_recv()
    rows_one[pl.ds(0, 1)] = video_sums(tms_one, inside, entries)
    row_sums = Rows(rows_one, 0)
    row_sums.start()
    halo_one.start_beside()

    @pl.when(exists(1))
    def _():
        pl.semaphore_wait(full, 1)

    halo_one.start_corners()
    load_vecs.wait()
    row_sums.all.wait_recv()
    stats = video_stats(rows_one, entries)
    halo_one.wait_recv()
    load_one.wait()
    results = convolved(raw, stats, vecs[0:1], vecs[1:2], taps_one)
    results = [[(y + vecs[2:3]).astype(jnp.bfloat16) for y in rows] for rows in results]
    for f in range(count):
        for i in range(height):
            mid[count + f, 1 + i] = results[f][i]
    rows_two[pl.ds(0, 1)] = local_stats(results)
    row_sums_two = Rows(rows_two, 1)
    row_sums_two.start()
    halo_two = Halo(mid, 1)
    halo_two.start_beside()
    halo_two.start_corners()
    halo_two.start_onward(0, 1)
    tm_sums.wait_send()
    row_sums.all.wait_send()
    halo_one.wait_send()

    row_sums_two.all.wait_recv()
    tms_two[pl.ds(0, 1)] = frame_sums(rows_two)
    tm_sums_two = Frames(tms_two, 1)
    tm_sums_two.start(-1, 1)
    tm_sums_two.wait_recv()
    stats = frame_stats(tms_two, inside, entries)
    halo_two.wait_recv()
    load_two.wait()
    results = convolved(mid, stats, vecs[3:4], vecs[4:5], taps_two)
    for f in range(count):
        for i in range(height):
            out[f, i] = results[f][i] + vecs[5:6] + raw[count + f, 1 + i].astype(jnp.float32)
    tm_sums_two.wait_send()
    row_sums_two.all.wait_send()
    halo_two.wait_send()


def per_device(n_tm, n_rows, *args):
    frames, lengths = args[0], args[1]
    count, height, cols, width = frames.shape
    near = len(tm_offsets(n_tm, count))
    window = -(-(1 + near) // 8) * 8
    block = pltpu.VMEM((2 * count, height + 2, cols, width), jnp.bfloat16)
    taps = pltpu.VMEM((3, 3, width, 3 * width), jnp.bfloat16)
    return pl.pallas_call(
        functools.partial(kernel, n_tm, n_rows),
        out_shape=pltpu.VMEM(frames.shape, jnp.float32),
        in_specs=[pl.BlockSpec(memory_space=pl.ANY)] * len(args),
        out_specs=pl.BlockSpec(memory_space=pltpu.VMEM),
        scratch_shapes=[
            block, block, taps, taps,
            pltpu.VMEM((8, width), jnp.float32),
            pltpu.SMEM(lengths.shape, jnp.int32),
            pltpu.VMEM((n_rows, width), jnp.float32),
            pltpu.VMEM((n_rows, width), jnp.float32),
            pltpu.VMEM((window, width), jnp.float32),
            pltpu.VMEM((window, width), jnp.float32),
            pltpu.SemaphoreType.REGULAR((3 + near // 2 + 1,)),
            pltpu.SemaphoreType.DMA((5,)),
            pltpu.SemaphoreType.DMA((2, 2)),
            pltpu.SemaphoreType.DMA((2, 2)),
            pltpu.SemaphoreType.DMA((2,)),
            pltpu.SemaphoreType.DMA((2,)),
            pltpu.SemaphoreType.DMA((2,)),
            pltpu.SemaphoreType.DMA((2,)),
        ],
        compiler_params=pltpu.CompilerParams(
            collective_id=0, has_side_effects=True, vmem_limit_bytes=40 * 1024 * 1024
        ),
        name="residual_block",
    )(*[pltpu.with_memory_space_constraint(a, pltpu.HBM) for a in args])


def solution(mesh):
    placed = (P("tm", "rows", None, None), P(), P(), P(), P(), P(), P(), P(), P(), P())
    return jax.shard_map(
        functools.partial(per_device, mesh.shape["tm"], mesh.shape["rows"]),
        mesh=mesh,
        in_specs=placed,
        out_specs=P("tm", "rows", None, None),
        check_vma=False,
    )
```

```python
import functools

import jax
import jax.numpy as jnp
from jax import lax
from jax.experimental import pallas as pl
from jax.experimental.pallas import tpu as pltpu
from jax.sharding import PartitionSpec as P

GROUPS = 32
MOST = 16
MESH = pl.DeviceIdType.MESH


def tm_offsets(n_tm, count):
    reach = min(-(-(MOST - 1) // count), n_tm - 1)
    return [d for far in range(1, reach + 1) for d in (far, -far)]


def tm_hops(d):
    return abs(d) // 4 + min(abs(d) % 4, 4 - abs(d) % 4)


def wrapped(index, offset, size):
    return lax.rem(index + (offset + size), size)


def neighbours(row):
    lanes = row.shape[1]
    return {s: pltpu.roll(row, s % lanes, 1) if s else row for s in range(-3, 4)}


def by_place(place, choices):
    picked = choices[-1]
    for i in range(len(choices) - 1):
        picked = jnp.where(place == i, choices[i], picked)
    return picked


def group_total(row, place):
    near = neighbours(row)
    sums = [near[i] + near[i - 1] + (near[i - 2] + near[i - 3]) for i in range(4)]
    return by_place(place, sums)


def await_signals(semaphore, number):
    @pl.when(number > 0)
    def _():
        pl.semaphore_wait(semaphore, number)


def kernel(
    n_tm, n_rows,
    frames, lengths, gain_one, shift_one, conv_one, bias_one, gain_two, shift_two, conv_two, bias_two,
    out,
    raw, mid, taps_one, taps_two, vecs, lens, rows_one, rows_two, tms_one, tms_two,
    ready, load_sem, halo_send, halo_recv, row_send, row_recv, tm_send, tm_recv,
):
    count, height, cols, width = frames.shape
    videos = lengths.shape[0]
    tm = lax.axis_index("tm")
    row = lax.axis_index("rows")
    first = tm * count
    offsets = tm_offsets(n_tm, count)

    load_frames = pltpu.make_async_copy(
        frames, raw.at[pl.ds(count, count), pl.ds(1, height)], load_sem.at[0]
    )
    load_frames.start()

    def exists(d):
        return (tm + d >= 0) & (tm + d < n_tm)

    def device(d, k):
        return {"tm": tm + d, "rows": wrapped(row, k, n_rows)}

    host = n_rows > 1 and 1
    hosting = row == host
    reach = max(offsets)
    below = jnp.minimum(tm, reach)
    above = jnp.minimum(n_tm - 1 - tm, reach)
    barrier = pltpu.get_barrier_semaphore()
    answers, complete = ready.at[0], ready.at[1]

    def signal(semaphore, target):
        pl.semaphore_signal(semaphore, inc=1, device_id=target, device_id_type=MESH)

    def tell_rows(semaphore):
        @pl.when(hosting)
        def _():
            for k in sorted(range(1, n_rows), key=lambda k: -min(k, n_rows - k)):
                signal(semaphore, device(0, k))

    for d in range(1, reach + 1):

        @pl.when(exists(d))
        def _(d=d):
            signal(barrier, device(d, 0))

    tell_rows(barrier)
    announced = below + jnp.where(hosting, 0, 1)

    def answer():
        for d in range(1, reach + 1):

            @pl.when(exists(-d))
            def _(d=d):
                signal(ready.at[1 + d], device(-d, 0))

        @pl.when(jnp.logical_not(hosting))
        def _():
            signal(answers, {"tm": tm, "rows": host})

    load_lens = pltpu.make_async_copy(lengths, lens, load_sem.at[1])
    load_lens.start()
    for i, vec in enumerate((gain_one, shift_one, bias_one, gain_two, shift_two, bias_two)):
        pltpu.make_async_copy(vec, vecs.at[i], load_sem.at[2]).start()
    for dx in range(3):
        for i, (source, held) in enumerate(((conv_one, taps_one), (conv_two, taps_two))):
            pltpu.make_async_copy(
                source.at[:, :, dx], held.at[:, :, :, pl.ds(dx * width, width)], load_sem.at[3 + i]
            ).start()
    load_vecs = pltpu.make_async_copy(vecs.at[pl.ds(0, 6)], vecs.at[pl.ds(0, 6)], load_sem.at[2])
    load_one = pltpu.make_async_copy(taps_one, taps_one, load_sem.at[3])
    load_two = pltpu.make_async_copy(taps_two, taps_two, load_sem.at[4])

    def remote(src, dst, send, recv, d, k):
        return pltpu.make_async_remote_copy(
            src_ref=src,
            dst_ref=dst,
            send_sem=send,
            recv_sem=recv,
            device_id=device(d, k),
            device_id_type=MESH,
        )

    class Halo:
        def __init__(self, block, half, passed):
            own, prior = pl.ds(count, count), pl.ds(0, count)
            whole, last, head = pl.ds(1, height), pl.ds(height, 1), pl.ds(1, 1)
            above, below = pl.ds(0, 1), pl.ds(height + 1, 1)

            def copy(f, src, g, dst, d, k):
                sems = halo_send.at[half, d], halo_recv.at[half, d]
                return remote(block.at[f, src], block.at[g, dst], *sems, d, k)

            self.beside = [copy(own, last, own, above, 0, 1), copy(own, head, own, below, 0, -1)]
            halves = [(pl.ds(count + f, 1), pl.ds(f, 1)) for f in range(count)]
            self.onward = [copy(src, whole, dst, whole, 1, 0) for src, dst in halves]
            if passed:
                self.corners = [copy(own, above, prior, above, 1, 0), copy(own, below, prior, below, 1, 0)]
            else:
                self.corners = [copy(own, last, prior, above, 1, 1), copy(own, head, prior, below, 1, -1)]
            edge = block.at[:, pl.ds(0, 1)]
            self.all_beside = remote(edge, edge, halo_send.at[half, 0], halo_recv.at[half, 0], 0, 1)
            front = block.at[prior]
            self.all_onward = remote(front, front, halo_send.at[half, 1], halo_recv.at[half, 1], 0, 1)

        def start_beside(self):
            for copy in self.beside:
                copy.start()

        def start_onward(self, *halves):
            @pl.when(exists(1))
            def _():
                for half in halves:
                    self.onward[half].start()

        def start_corners(self):
            @pl.when(exists(1))
            def _():
                for copy in self.corners:
                    copy.start()

        def wait_onward(self):
            pl.when(exists(-1))(self.all_onward.wait_recv)

        def wait_send(self):
            self.all_beside.wait_send()
            pl.when(exists(1))(self.all_onward.wait_send)

    class Rows:
        def __init__(self, slots, half):
            sems = row_send.at[half], row_recv.at[half]
            self.copies = [
                remote(slots.at[pl.ds(0, 1)], slots.at[pl.ds(k, 1)], *sems, 0, k) for k in range(1, n_rows)
            ]
            others = slots.at[pl.ds(1, n_rows - 1)]
            self.all = remote(others, others, *sems, 0, 1)

        def start(self):
            for k in sorted(range(1, n_rows), key=lambda k: -min(k, n_rows - k)):
                self.copies[k - 1].start()

    class Frames:
        def __init__(self, slots, half):
            sems = tm_send.at[half], tm_recv.at[half]
            self.copies = {
                d: remote(slots.at[pl.ds(0, 1)], slots.at[pl.ds(1 + i, 1)], *sems, d, 0)
                for i, d in enumerate(offsets)
            }
            self.all = {}
            for n in range(reach, 2 * reach + 1):
                others = slots.at[pl.ds(1, n)]
                self.all[n] = remote(others, others, *sems, 0, 1)

        def start(self, *signs):
            for d in sorted(range(1, reach + 1), key=lambda d: -tm_hops(d)):
                for sign in signs:
                    pl.when(exists(sign * d))(self.copies[sign * d].start)

        def wait_recv(self):
            for n in self.all:
                pl.when(below + above == n)(self.all[n].wait_recv)

        def wait_send(self):
            for n in self.all:
                pl.when(below + above == n)(self.all[n].wait_send)

    members = width // GROUPS
    per_block = float(height * cols * members)
    place = lax.rem(lax.broadcasted_iota(jnp.int32, (1, width), 1), members)
    odd = lax.rem(place, 2) == 1
    head = place < 2

    def local_stats(frames_rows):
        totals, squares = [], []
        for rows in frames_rows:
            near = jnp.sum(rows[0].astype(jnp.float32), axis=0, keepdims=True) * (1.0 / cols)
            first_sum = jnp.zeros((cols, width), jnp.float32)
            second_sum = jnp.zeros((cols, width), jnp.float32)
            for values in rows:
                off = values.astype(jnp.float32) - near
                first_sum = first_sum + off
                second_sum = second_sum + off * off
            first_sum = jnp.sum(first_sum, axis=0, keepdims=True)
            second_sum = jnp.sum(second_sum, axis=0, keepdims=True)
            shift = first_sum * (1.0 / (height * cols))
            total = group_total(first_sum + near * float(height * cols), place)
            off = near + shift - total * (1.0 / per_block)
            square = second_sum - first_sum * shift + off * off * float(height * cols)
            totals.append(total)
            squares.append(group_total(square, place))
        return by_place(place, totals + squares)

    def video_sums(slots, inside, entries):
        parts = slots[...]
        merged = []
        for f in range(count):
            total = jnp.sum(jnp.where(inside[f], parts, 0.0), axis=0, keepdims=True)
            total = total + jnp.where(odd, pltpu.roll(total, 1, 1), pltpu.roll(total, width - 1, 1))
            off = parts * (1.0 / per_block) - total * (1.0 / entries[f])
            between = jnp.sum(jnp.where(inside[f], off * off, 0.0), axis=0, keepdims=True) * per_block
            between = pltpu.roll(between, 2, 1) + jnp.where(
                odd, pltpu.roll(between, 3, 1), pltpu.roll(between, 1, 1)
            )
            merged.append(total + jnp.where(head, 0.0, between))
        return jnp.where(odd, merged[1], merged[0])

    def video_stats(slots, entries):
        parts = slots[...]
        share = jnp.where(odd, entries[1], entries[0])
        total = jnp.sum(parts, axis=0, keepdims=True)
        mean = total / (share * n_rows)
        off = parts * (1.0 / share) - mean
        between = jnp.sum(off * off, axis=0, keepdims=True) * share
        var = (total + pltpu.roll(between, 2, 1)) / (share * n_rows)
        near = neighbours(jnp.where(head, mean, lax.rsqrt(var + 1e-6)))
        spread = [by_place(place, [near[i - k] for i in range(4)]) for k in range(4)]
        return [(spread[f], spread[count + f]) for f in range(count)]

    column = lax.broadcasted_iota(jnp.int32, (cols, width), 0)

    def convolved(block, stats, gain, shift, taps):
        def active(f, i, moved):
            mean, scale = stats[max(f - count, 0)]
            v = (block[f, i].astype(jnp.float32) - mean) * (scale * gain) + shift
            v = v * (0.5 * jnp.tanh(0.5 * v) + 0.5)
            if i == 0:
                v = jnp.where(row == 0, 0.0, v)
            if i == height + 1:
                v = jnp.where(row == n_rows - 1, 0.0, v)
            if moved:
                moved = jnp.where(column == cols - 1, 0.0, pltpu.roll(v, cols - 1, 0))
                return v.astype(jnp.bfloat16), moved.astype(jnp.bfloat16)
            return v.astype(jnp.bfloat16)

        seen = [[[], [], []] for _ in range(count)]
        moved = [[], []]
        for i in range(height + 2):
            a, b = active(0, i, False), active(1, i, False)
            c, d = active(2, i, i >= 2), active(3, i, i >= 2)
            if i >= 2:
                c, moved_c = c
                d, moved_d = d
                moved[0].append(moved_c)
                moved[1].append(moved_d)
            b = jnp.where(starts[0] < first, b, c)
            seen[0][0].append(jnp.where(starts[0] < first - 1, a, b))
            seen[0][1].append(b)
            seen[0][2].append(c)
            seen[1][0].append(jnp.where(starts[1] > first, d, b))
            seen[1][1].append(jnp.where(starts[1] > first, d, c))
            seen[1][2].append(d)
        right = taps[...].reshape(9 * width, 3 * width)[: 8 * width]
        ninth = taps[2, 2]
        blank = jnp.zeros((width, width), jnp.bfloat16)
        ninth = jnp.concatenate(
            [ninth[:, : 2 * width], jnp.concatenate([blank, ninth[:, 2 * width :]], axis=1)], axis=0
        )
        results = []
        for f in range(count):
            pieces = [
                jnp.concatenate(seen[f][dt][dy : dy + height], axis=0) for dt in range(3) for dy in range(3)
            ]
            wide = jnp.dot(jnp.concatenate(pieces[:8], axis=1), right, preferred_element_type=jnp.float32)
            last = jnp.concatenate([pieces[8], jnp.concatenate(moved[f], axis=0)], axis=1)
            last = jnp.dot(last, ninth, preferred_element_type=jnp.float32)
            rows = []
            for i in range(height):
                y = wide[i * cols : (i + 1) * cols]
                z = last[i * cols : (i + 1) * cols]
                before = pltpu.roll(y[:, :width] + z[:, :width], 1, 0)
                after = pltpu.roll(y[:, 2 * width :], cols - 1, 0)
                rows.append(
                    y[:, width : 2 * width]
                    + z[:, width:]
                    + jnp.where(column == 0, 0.0, before)
                    + jnp.where(column == cols - 1, 0.0, after)
                )
            results.append(rows)
        return results

    def frame_sums(slots):
        parts = slots[...]
        total = jnp.sum(parts, axis=0, keepdims=True)
        off = parts * (1.0 / per_block) - total * (1.0 / (per_block * n_rows))
        between = jnp.sum(off * off, axis=0, keepdims=True) * per_block
        return total + jnp.where(head, 0.0, pltpu.roll(between, 2, 1))

    def frame_stats(slots, inside, entries):
        parts = slots[...]
        per_frame = per_block * n_rows
        stats = []
        for f in range(count):
            total = jnp.sum(jnp.where(inside[f], parts, 0.0), axis=0, keepdims=True)
            mean = group_total(jnp.where(head, total, 0.0), place) / (entries[f] * n_rows)
            off = parts * (1.0 / per_frame) - mean
            between = jnp.sum(jnp.where(inside[f], off * off, 0.0), axis=0, keepdims=True) * per_frame
            var = group_total(jnp.where(head, between, total), place) / (entries[f] * n_rows)
            stats.append((mean, lax.rsqrt(var + 1e-6)))
        return stats

    await_signals(barrier, announced)
    answer()
    load_frames.wait()
    tms_one[pl.ds(0, 1)] = local_stats(
        [[raw[count + f, 1 + i] for i in range(height)] for f in range(count)]
    )
    tm_sums = Frames(tms_one, 0)
    tm_sums.start(-1)

    load_lens.wait()
    starts, stops = [], []
    for f in range(count):
        start = jnp.int32(0)
        stop = jnp.int32(0)
        offset = jnp.int32(0)
        for v in range(videos):
            size = lens[v]
            here = offset <= first + f
            start = jnp.where(here, offset, start)
            stop = jnp.where(here, offset + size, stop)
            offset = offset + size
        starts.append(start)
        stops.append(stop)
    entries = [(stops[f] - starts[f]).astype(jnp.float32) * per_block for f in range(count)]
    slot = lax.broadcasted_iota(jnp.int32, tms_one.shape, 0)
    lane = lax.broadcasted_iota(jnp.int32, tms_one.shape, 1)
    far = (slot + 1) // 2
    home = tm - jnp.where(lax.rem(slot, 2) == 1, far, -far)
    frame = home * count + lax.rem(lane, count)
    known = slot <= len(offsets)
    inside = [known & (frame >= starts[f]) & (frame < stops[f]) for f in range(count)]

    halo_one = Halo(raw, 0, passed=True)
    for d in range(1, reach + 1):

        @pl.when(exists(d))
        def _(d=d):
            pl.semaphore_wait(ready.at[1 + d], 1)
            tm_sums.copies[d].start()

        if d == reach // 2:
            halo_one.start_onward(0)

    halo_one.start_onward(1)

    @pl.when(hosting)
    def _():
        pl.semaphore_wait(answers, n_rows - 1)

    tell_rows(complete)

    @pl.when(jnp.logical_not(hosting))
    def _():
        pl.semaphore_wait(complete, 1)

    halo_one.start_beside()
    tm_sums.wait_recv()
    rows_one[pl.ds(0, 1)] = video_sums(tms_one, inside, entries)
    row_sums = Rows(rows_one, 0)
    row_sums.start()
    halo_one.all_beside.wait_recv()
    halo_one.start_corners()
    load_vecs.wait()
    row_sums.all.wait_recv()
    stats = video_stats(rows_one, entries)
    halo_one.wait_onward()
    load_one.wait()
    results = convolved(raw, stats, vecs[0:1], vecs[1:2], taps_one)
    results = [[(y + vecs[2:3]).astype(jnp.bfloat16) for y in rows] for rows in results]
    for f in range(count):
        for i in range(height):
            mid[count + f, 1 + i] = results[f][i]
    rows_two[pl.ds(0, 1)] = local_stats(results)
    row_sums_two = Rows(rows_two, 1)
    row_sums_two.start()
    halo_two = Halo(mid, 1, passed=False)
    halo_two.start_beside()
    halo_two.start_corners()
    halo_two.start_onward(0, 1)
    tm_sums.wait_send()
    row_sums.all.wait_send()
    halo_one.wait_send()

    row_sums_two.all.wait_recv()
    tms_two[pl.ds(0, 1)] = frame_sums(rows_two)
    tm_sums_two = Frames(tms_two, 1)
    tm_sums_two.start(-1, 1)
    tm_sums_two.wait_recv()
    stats = frame_stats(tms_two, inside, entries)
    halo_two.all_beside.wait_recv()
    halo_two.wait_onward()
    load_two.wait()
    results = convolved(mid, stats, vecs[3:4], vecs[4:5], taps_two)
    for f in range(count):
        for i in range(height):
            out[f, i] = results[f][i] + vecs[5:6] + raw[count + f, 1 + i].astype(jnp.float32)
    tm_sums_two.wait_send()
    row_sums_two.all.wait_send()
    halo_two.wait_send()


def per_device(n_tm, n_rows, *args):
    frames, lengths = args[0], args[1]
    count, height, cols, width = frames.shape
    near = len(tm_offsets(n_tm, count))
    window = -(-(1 + near) // 8) * 8
    block = pltpu.VMEM((2 * count, height + 2, cols, width), jnp.bfloat16)
    taps = pltpu.VMEM((3, 3, width, 3 * width), jnp.bfloat16)
    return pl.pallas_call(
        functools.partial(kernel, n_tm, n_rows),
        out_shape=pltpu.VMEM(frames.shape, jnp.float32),
        in_specs=[pl.BlockSpec(memory_space=pl.ANY)] * len(args),
        out_specs=pl.BlockSpec(memory_space=pltpu.VMEM),
        scratch_shapes=[
            block, block, taps, taps,
            pltpu.VMEM((8, width), jnp.float32),
            pltpu.SMEM(lengths.shape, jnp.int32),
            pltpu.VMEM((n_rows, width), jnp.float32),
            pltpu.VMEM((n_rows, width), jnp.float32),
            pltpu.VMEM((window, width), jnp.float32),
            pltpu.VMEM((window, width), jnp.float32),
            pltpu.SemaphoreType.REGULAR((2 + near // 2,)),
            pltpu.SemaphoreType.DMA((5,)),
            pltpu.SemaphoreType.DMA((2, 2)),
            pltpu.SemaphoreType.DMA((2, 2)),
            pltpu.SemaphoreType.DMA((2,)),
            pltpu.SemaphoreType.DMA((2,)),
            pltpu.SemaphoreType.DMA((2,)),
            pltpu.SemaphoreType.DMA((2,)),
        ],
        compiler_params=pltpu.CompilerParams(
            collective_id=0, has_side_effects=True, vmem_limit_bytes=40 * 1024 * 1024
        ),
        name="residual_block",
    )(*[pltpu.with_memory_space_constraint(a, pltpu.HBM) for a in args])


def solution(mesh):
    placed = (P("tm", "rows", None, None), P(), P(), P(), P(), P(), P(), P(), P(), P())
    return jax.shard_map(
        functools.partial(per_device, mesh.shape["tm"], mesh.shape["rows"]),
        mesh=mesh,
        in_specs=placed,
        out_specs=P("tm", "rows", None, None),
        check_vma=False,
    )
```

```python
import functools

import jax
import jax.numpy as jnp
from jax import lax
from jax.experimental import pallas as pl
from jax.experimental.pallas import tpu as pltpu
from jax.sharding import PartitionSpec as P

GROUPS = 32
MOST = 16
MESH = pl.DeviceIdType.MESH


def tm_offsets(n_tm, count):
    reach = min(-(-(MOST - 1) // count), n_tm - 1)
    return [d for far in range(1, reach + 1) for d in (far, -far)]


def tm_hops(d):
    return abs(d) // 4 + min(abs(d) % 4, 4 - abs(d) % 4)


def wrapped(index, offset, size):
    return lax.rem(index + (offset + size), size)


def neighbours(row):
    lanes = row.shape[1]
    return {s: pltpu.roll(row, s % lanes, 1) if s else row for s in range(-3, 4)}


def by_place(place, choices):
    picked = choices[-1]
    for i in range(len(choices) - 1):
        picked = jnp.where(place == i, choices[i], picked)
    return picked


def group_total(row, place):
    near = neighbours(row)
    sums = [near[i] + near[i - 1] + (near[i - 2] + near[i - 3]) for i in range(4)]
    return by_place(place, sums)


def await_signals(semaphore, number):
    @pl.when(number > 0)
    def _():
        pl.semaphore_wait(semaphore, number)


def kernel(
    n_tm, n_rows,
    frames, lengths, gain_one, shift_one, conv_one, bias_one, gain_two, shift_two, conv_two, bias_two,
    out,
    raw, mid, taps_one, taps_two, vecs, lens, rows_one, rows_two, tms_one, tms_two,
    ready, load_sem, halo_send, halo_recv, row_send, row_recv, tm_send, tm_recv,
):
    count, height, cols, width = frames.shape
    videos = lengths.shape[0]
    tm = lax.axis_index("tm")
    row = lax.axis_index("rows")
    first = tm * count
    offsets = tm_offsets(n_tm, count)

    load_frames = pltpu.make_async_copy(
        frames, raw.at[pl.ds(count, count), pl.ds(1, height)], load_sem.at[0]
    )
    load_frames.start()

    def exists(d):
        return (tm + d >= 0) & (tm + d < n_tm)

    def device(d, k):
        return {"tm": tm + d, "rows": wrapped(row, k, n_rows)}

    host = n_rows > 1 and 1
    hosting = row == host
    reach = max(offsets)
    below = jnp.minimum(tm, reach)
    above = jnp.minimum(n_tm - 1 - tm, reach)
    barrier = pltpu.get_barrier_semaphore()
    answers, complete = ready.at[0], ready.at[1]

    def signal(semaphore, target):
        pl.semaphore_signal(semaphore, inc=1, device_id=target, device_id_type=MESH)

    def tell_rows(semaphore):
        @pl.when(hosting)
        def _():
            for k in sorted(range(1, n_rows), key=lambda k: -min(k, n_rows - k)):
                signal(semaphore, device(0, k))

    for d in range(1, reach + 1):

        @pl.when(exists(d))
        def _(d=d):
            signal(barrier, device(d, 0))

    tell_rows(barrier)
    announced = below + jnp.where(hosting, 0, 1)

    def answer():
        for d in range(1, reach + 1):

            @pl.when(exists(-d))
            def _(d=d):
                signal(ready.at[1 + d], device(-d, 0))

        @pl.when(jnp.logical_not(hosting))
        def _():
            signal(answers, {"tm": tm, "rows": host})

    load_lens = pltpu.make_async_copy(lengths, lens, load_sem.at[1])
    load_lens.start()
    for i, vec in enumerate((gain_one, shift_one, bias_one, gain_two, shift_two, bias_two)):
        pltpu.make_async_copy(vec, vecs.at[i], load_sem.at[2]).start()
    for dx in range(3):
        for i, (source, held) in enumerate(((conv_one, taps_one), (conv_two, taps_two))):
            pltpu.make_async_copy(
                source.at[:, :, dx], held.at[:, :, :, pl.ds(dx * width, width)], load_sem.at[3 + i]
            ).start()
    load_vecs = pltpu.make_async_copy(vecs.at[pl.ds(0, 6)], vecs.at[pl.ds(0, 6)], load_sem.at[2])
    load_one = pltpu.make_async_copy(taps_one, taps_one, load_sem.at[3])
    load_two = pltpu.make_async_copy(taps_two, taps_two, load_sem.at[4])

    def remote(src, dst, send, recv, d, k):
        return pltpu.make_async_remote_copy(
            src_ref=src,
            dst_ref=dst,
            send_sem=send,
            recv_sem=recv,
            device_id=device(d, k),
            device_id_type=MESH,
        )

    class Halo:
        def __init__(self, block, half, passed):
            own, prior = pl.ds(count, count), pl.ds(0, count)
            whole, last, head = pl.ds(1, height), pl.ds(height, 1), pl.ds(1, 1)
            above, below = pl.ds(0, 1), pl.ds(height + 1, 1)

            def copy(f, src, g, dst, d, k):
                sems = halo_send.at[half, d], halo_recv.at[half, d]
                return remote(block.at[f, src], block.at[g, dst], *sems, d, k)

            self.beside = [copy(own, last, own, above, 0, 1), copy(own, head, own, below, 0, -1)]
            halves = [(pl.ds(count + f, 1), pl.ds(f, 1)) for f in range(count)]
            self.onward = [copy(src, whole, dst, whole, 1, 0) for src, dst in halves]
            if passed:
                self.corners = [copy(own, above, prior, above, 1, 0), copy(own, below, prior, below, 1, 0)]
            else:
                self.corners = [copy(own, last, prior, above, 1, 1), copy(own, head, prior, below, 1, -1)]
            edge = block.at[:, pl.ds(0, 1)]
            self.all_beside = remote(edge, edge, halo_send.at[half, 0], halo_recv.at[half, 0], 0, 1)
            front = block.at[prior]
            self.all_onward = remote(front, front, halo_send.at[half, 1], halo_recv.at[half, 1], 0, 1)

        def start_beside(self):
            for copy in self.beside:
                copy.start()

        def start_onward(self, *halves):
            @pl.when(exists(1))
            def _():
                for half in halves:
                    self.onward[half].start()

        def start_corners(self):
            @pl.when(exists(1))
            def _():
                for copy in self.corners:
                    copy.start()

        def wait_onward(self):
            pl.when(exists(-1))(self.all_onward.wait_recv)

        def wait_send(self):
            self.all_beside.wait_send()
            pl.when(exists(1))(self.all_onward.wait_send)

    class Rows:
        def __init__(self, slots, half):
            sems = row_send.at[half], row_recv.at[half]
            self.copies = [
                remote(slots.at[pl.ds(0, 1)], slots.at[pl.ds(k, 1)], *sems, 0, k) for k in range(1, n_rows)
            ]
            others = slots.at[pl.ds(1, n_rows - 1)]
            self.all = remote(others, others, *sems, 0, 1)

        def start(self):
            for k in sorted(range(1, n_rows), key=lambda k: -min(k, n_rows - k)):
                self.copies[k - 1].start()

    class Frames:
        def __init__(self, slots, half):
            sems = tm_send.at[half], tm_recv.at[half]
            self.copies = {
                d: remote(slots.at[pl.ds(0, 1)], slots.at[pl.ds(1 + i, 1)], *sems, d, 0)
                for i, d in enumerate(offsets)
            }
            self.all = {}
            for n in range(reach, 2 * reach + 1):
                others = slots.at[pl.ds(1, n)]
                self.all[n] = remote(others, others, *sems, 0, 1)

        def start(self, *signs):
            for d in sorted(range(1, reach + 1), key=lambda d: -tm_hops(d)):
                for sign in signs:
                    pl.when(exists(sign * d))(self.copies[sign * d].start)

        def wait_recv(self):
            for n in self.all:
                pl.when(below + above == n)(self.all[n].wait_recv)

        def wait_send(self):
            for n in self.all:
                pl.when(below + above == n)(self.all[n].wait_send)

    members = width // GROUPS
    per_block = float(height * cols * members)
    place = lax.rem(lax.broadcasted_iota(jnp.int32, (1, width), 1), members)
    odd = lax.rem(place, 2) == 1
    head = place < 2

    def local_stats(frames_rows):
        totals, squares = [], []
        for rows in frames_rows:
            near = jnp.sum(rows[0].astype(jnp.float32), axis=0, keepdims=True) * (1.0 / cols)
            first_sum = jnp.zeros((cols, width), jnp.float32)
            second_sum = jnp.zeros((cols, width), jnp.float32)
            for values in rows:
                off = values.astype(jnp.float32) - near
                first_sum = first_sum + off
                second_sum = second_sum + off * off
            first_sum = jnp.sum(first_sum, axis=0, keepdims=True)
            second_sum = jnp.sum(second_sum, axis=0, keepdims=True)
            shift = first_sum * (1.0 / (height * cols))
            total = group_total(first_sum + near * float(height * cols), place)
            off = near + shift - total * (1.0 / per_block)
            square = second_sum - first_sum * shift + off * off * float(height * cols)
            totals.append(total)
            squares.append(group_total(square, place))
        return by_place(place, totals + squares)

    def video_sums(slots, inside, shares):
        parts = slots[...]
        merged = []
        for f in range(count):
            total = jnp.sum(jnp.where(inside[f], parts, 0.0), axis=0, keepdims=True)
            total = total + jnp.where(odd, pltpu.roll(total, 1, 1), pltpu.roll(total, width - 1, 1))
            off = parts * (1.0 / per_block) - total * shares[f]
            between = jnp.sum(jnp.where(inside[f], off * off, 0.0), axis=0, keepdims=True) * per_block
            between = pltpu.roll(between, 2, 1) + jnp.where(
                odd, pltpu.roll(between, 3, 1), pltpu.roll(between, 1, 1)
            )
            merged.append(total + jnp.where(head, 0.0, between))
        return jnp.where(odd, merged[1], merged[0])

    def video_stats(slots, held, share):
        parts = slots[...]
        total = jnp.sum(parts, axis=0, keepdims=True)
        mean = total * share * (1.0 / n_rows)
        off = parts * share - mean
        between = jnp.sum(off * off, axis=0, keepdims=True) * held
        var = (total + pltpu.roll(between, 2, 1)) * share * (1.0 / n_rows)
        near = neighbours(jnp.where(head, mean, lax.rsqrt(var + 1e-6)))
        spread = [by_place(place, [near[i - k] for i in range(4)]) for k in range(4)]
        return [(spread[f], spread[count + f]) for f in range(count)]

    column = lax.broadcasted_iota(jnp.int32, (cols, width), 0)

    def convolved(block, stats, gain, shift, taps):
        def active(f, i, moved):
            mean, scale = stats[max(f - count, 0)]
            v = (block[f, i].astype(jnp.float32) - mean) * (scale * gain) + shift
            v = v * (0.5 * jnp.tanh(0.5 * v) + 0.5)
            if i == 0:
                v = jnp.where(row == 0, 0.0, v)
            if i == height + 1:
                v = jnp.where(row == n_rows - 1, 0.0, v)
            if moved:
                moved = jnp.where(column == cols - 1, 0.0, pltpu.roll(v, cols - 1, 0))
                return v.astype(jnp.bfloat16), moved.astype(jnp.bfloat16)
            return v.astype(jnp.bfloat16)

        seen = [[[], [], []] for _ in range(count)]
        moved = [[], []]
        for i in range(height + 2):
            a, b = active(0, i, False), active(1, i, False)
            c, d = active(2, i, i >= 2), active(3, i, i >= 2)
            if i >= 2:
                c, moved_c = c
                d, moved_d = d
                moved[0].append(moved_c)
                moved[1].append(moved_d)
            b = jnp.where(starts[0] < first, b, c)
            seen[0][0].append(jnp.where(starts[0] < first - 1, a, b))
            seen[0][1].append(b)
            seen[0][2].append(c)
            seen[1][0].append(jnp.where(starts[1] > first, d, b))
            seen[1][1].append(jnp.where(starts[1] > first, d, c))
            seen[1][2].append(d)
        right = taps[...].reshape(9 * width, 3 * width)[: 8 * width]
        ninth = taps[2, 2]
        blank = jnp.zeros((width, width), jnp.bfloat16)
        ninth = jnp.concatenate(
            [ninth[:, : 2 * width], jnp.concatenate([blank, ninth[:, 2 * width :]], axis=1)], axis=0
        )
        results = []
        for f in range(count):
            pieces = [
                jnp.concatenate(seen[f][dt][dy : dy + height], axis=0) for dt in range(3) for dy in range(3)
            ]
            wide = jnp.dot(jnp.concatenate(pieces[:8], axis=1), right, preferred_element_type=jnp.float32)
            last = jnp.concatenate([pieces[8], jnp.concatenate(moved[f], axis=0)], axis=1)
            last = jnp.dot(last, ninth, preferred_element_type=jnp.float32)
            rows = []
            for i in range(height):
                y = wide[i * cols : (i + 1) * cols]
                z = last[i * cols : (i + 1) * cols]
                before = pltpu.roll(y[:, :width] + z[:, :width], 1, 0)
                after = pltpu.roll(y[:, 2 * width :], cols - 1, 0)
                rows.append(
                    y[:, width : 2 * width]
                    + z[:, width:]
                    + jnp.where(column == 0, 0.0, before)
                    + jnp.where(column == cols - 1, 0.0, after)
                )
            results.append(rows)
        return results

    def frame_sums(slots):
        parts = slots[...]
        total = jnp.sum(parts, axis=0, keepdims=True)
        off = parts * (1.0 / per_block) - total * (1.0 / (per_block * n_rows))
        between = jnp.sum(off * off, axis=0, keepdims=True) * per_block
        return total + jnp.where(head, 0.0, pltpu.roll(between, 2, 1))

    def frame_stats(slots, inside, shares):
        parts = slots[...]
        per_frame = per_block * n_rows
        stats = []
        for f in range(count):
            total = jnp.sum(jnp.where(inside[f], parts, 0.0), axis=0, keepdims=True)
            mean = group_total(jnp.where(head, total, 0.0), place) * (shares[f] * (1.0 / n_rows))
            off = parts * (1.0 / per_frame) - mean
            between = jnp.sum(jnp.where(inside[f], off * off, 0.0), axis=0, keepdims=True) * per_frame
            var = group_total(jnp.where(head, between, total), place) * (shares[f] * (1.0 / n_rows))
            stats.append((mean, lax.rsqrt(var + 1e-6)))
        return stats

    await_signals(barrier, announced)
    answer()
    load_frames.wait()
    tms_one[pl.ds(0, 1)] = local_stats(
        [[raw[count + f, 1 + i] for i in range(height)] for f in range(count)]
    )
    tm_sums = Frames(tms_one, 0)
    tm_sums.start(-1)

    load_lens.wait()
    starts, stops = [], []
    for f in range(count):
        start = jnp.int32(0)
        stop = jnp.int32(0)
        offset = jnp.int32(0)
        for v in range(videos):
            size = lens[v]
            here = offset <= first + f
            start = jnp.where(here, offset, start)
            stop = jnp.where(here, offset + size, stop)
            offset = offset + size
        starts.append(start)
        stops.append(stop)
    entries = [(stops[f] - starts[f]).astype(jnp.float32) * per_block for f in range(count)]
    shares = [1.0 / jnp.full((1, width), entries[f], jnp.float32) for f in range(count)]
    held = jnp.where(odd, entries[1], entries[0])
    share = jnp.where(odd, shares[1], shares[0])
    slot = lax.broadcasted_iota(jnp.int32, tms_one.shape, 0)
    lane = lax.broadcasted_iota(jnp.int32, tms_one.shape, 1)
    far = (slot + 1) // 2
    home = tm - jnp.where(lax.rem(slot, 2) == 1, far, -far)
    frame = home * count + lax.rem(lane, count)
    known = slot <= len(offsets)
    inside = [known & (frame >= starts[f]) & (frame < stops[f]) for f in range(count)]

    halo_one = Halo(raw, 0, passed=True)
    for d in range(1, reach + 1):

        @pl.when(exists(d))
        def _(d=d):
            pl.semaphore_wait(ready.at[1 + d], 1)
            tm_sums.copies[d].start()

        if d == reach // 2:
            halo_one.start_onward(0)

    halo_one.start_onward(1)

    @pl.when(hosting)
    def _():
        pl.semaphore_wait(answers, n_rows - 1)

    tell_rows(complete)

    @pl.when(jnp.logical_not(hosting))
    def _():
        pl.semaphore_wait(complete, 1)

    halo_one.start_beside()
    tm_sums.wait_recv()
    rows_one[pl.ds(0, 1)] = video_sums(tms_one, inside, shares)
    row_sums = Rows(rows_one, 0)
    row_sums.start()
    halo_one.all_beside.wait_recv()
    halo_one.start_corners()
    load_vecs.wait()
    row_sums.all.wait_recv()
    stats = video_stats(rows_one, held, share)
    halo_one.wait_onward()
    load_one.wait()
    results = convolved(raw, stats, vecs[0:1], vecs[1:2], taps_one)
    results = [[(y + vecs[2:3]).astype(jnp.bfloat16) for y in rows] for rows in results]
    for f in range(count):
        for i in range(height):
            mid[count + f, 1 + i] = results[f][i]
    rows_two[pl.ds(0, 1)] = local_stats(results)
    row_sums_two = Rows(rows_two, 1)
    row_sums_two.start()
    halo_two = Halo(mid, 1, passed=False)
    halo_two.start_beside()
    halo_two.start_corners()
    halo_two.start_onward(0, 1)
    tm_sums.wait_send()
    row_sums.all.wait_send()
    halo_one.wait_send()

    row_sums_two.all.wait_recv()
    tms_two[pl.ds(0, 1)] = frame_sums(rows_two)
    tm_sums_two = Frames(tms_two, 1)
    tm_sums_two.start(-1, 1)
    tm_sums_two.wait_recv()
    stats = frame_stats(tms_two, inside, shares)
    halo_two.all_beside.wait_recv()
    halo_two.wait_onward()
    load_two.wait()
    results = convolved(mid, stats, vecs[3:4], vecs[4:5], taps_two)
    for f in range(count):
        for i in range(height):
            out[f, i] = results[f][i] + vecs[5:6] + raw[count + f, 1 + i].astype(jnp.float32)
    tm_sums_two.wait_send()
    row_sums_two.all.wait_send()
    halo_two.wait_send()


def per_device(n_tm, n_rows, *args):
    frames, lengths = args[0], args[1]
    count, height, cols, width = frames.shape
    near = len(tm_offsets(n_tm, count))
    window = -(-(1 + near) // 8) * 8
    block = pltpu.VMEM((2 * count, height + 2, cols, width), jnp.bfloat16)
    taps = pltpu.VMEM((3, 3, width, 3 * width), jnp.bfloat16)
    return pl.pallas_call(
        functools.partial(kernel, n_tm, n_rows),
        out_shape=pltpu.VMEM(frames.shape, jnp.float32),
        in_specs=[pl.BlockSpec(memory_space=pl.ANY)] * len(args),
        out_specs=pl.BlockSpec(memory_space=pltpu.VMEM),
        scratch_shapes=[
            block, block, taps, taps,
            pltpu.VMEM((8, width), jnp.float32),
            pltpu.SMEM(lengths.shape, jnp.int32),
            pltpu.VMEM((n_rows, width), jnp.float32),
            pltpu.VMEM((n_rows, width), jnp.float32),
            pltpu.VMEM((window, width), jnp.float32),
            pltpu.VMEM((window, width), jnp.float32),
            pltpu.SemaphoreType.REGULAR((2 + near // 2,)),
            pltpu.SemaphoreType.DMA((5,)),
            pltpu.SemaphoreType.DMA((2, 2)),
            pltpu.SemaphoreType.DMA((2, 2)),
            pltpu.SemaphoreType.DMA((2,)),
            pltpu.SemaphoreType.DMA((2,)),
            pltpu.SemaphoreType.DMA((2,)),
            pltpu.SemaphoreType.DMA((2,)),
        ],
        compiler_params=pltpu.CompilerParams(
            collective_id=0, has_side_effects=True, vmem_limit_bytes=40 * 1024 * 1024
        ),
        name="residual_block",
    )(*[pltpu.with_memory_space_constraint(a, pltpu.HBM) for a in args])


def solution(mesh):
    placed = (P("tm", "rows", None, None), P(), P(), P(), P(), P(), P(), P(), P(), P())
    return jax.shard_map(
        functools.partial(per_device, mesh.shape["tm"], mesh.shape["rows"]),
        mesh=mesh,
        in_specs=placed,
        out_specs=P("tm", "rows", None, None),
        check_vma=False,
    )
```

```python
import functools

import jax
import jax.numpy as jnp
from jax import lax
from jax.experimental import pallas as pl
from jax.experimental.pallas import tpu as pltpu
from jax.sharding import PartitionSpec as P

GROUPS = 32
MOST = 16
MESH = pl.DeviceIdType.MESH


def tm_offsets(n_tm, count):
    reach = min(-(-(MOST - 1) // count), n_tm - 1)
    return [d for far in range(1, reach + 1) for d in (far, -far)]


def tm_hops(d):
    return abs(d) // 4 + min(abs(d) % 4, 4 - abs(d) % 4)


def wrapped(index, offset, size):
    return lax.rem(index + (offset + size), size)


def neighbours(row):
    lanes = row.shape[1]
    return {s: pltpu.roll(row, s % lanes, 1) if s else row for s in range(-3, 4)}


def by_place(place, choices):
    picked = choices[-1]
    for i in range(len(choices) - 1):
        picked = jnp.where(place == i, choices[i], picked)
    return picked


def group_total(row, place):
    near = neighbours(row)
    sums = [near[i] + near[i - 1] + (near[i - 2] + near[i - 3]) for i in range(4)]
    return by_place(place, sums)


def await_signals(semaphore, number):
    @pl.when(number > 0)
    def _():
        pl.semaphore_wait(semaphore, number)


def kernel(
    n_tm, n_rows,
    frames, lengths, gain_one, shift_one, conv_one, bias_one, gain_two, shift_two, conv_two, bias_two,
    out,
    raw, mid, taps_one, taps_two, vecs, lens, rows_one, rows_two, tms_one, tms_two,
    ready, load_sem, halo_send, halo_recv, row_send, row_recv, tm_send, tm_recv,
):
    count, height, cols, width = frames.shape
    videos = lengths.shape[0]
    tm = lax.axis_index("tm")
    row = lax.axis_index("rows")
    first = tm * count
    offsets = tm_offsets(n_tm, count)

    load_frames = pltpu.make_async_copy(
        frames, raw.at[pl.ds(count, count), pl.ds(1, height)], load_sem.at[0]
    )
    load_frames.start()

    def exists(d):
        return (tm + d >= 0) & (tm + d < n_tm)

    def device(d, k):
        return {"tm": tm + d, "rows": wrapped(row, k, n_rows)}

    host = n_rows > 1 and 1
    hosting = row == host
    reach = max(offsets)
    below = jnp.minimum(tm, reach)
    above = jnp.minimum(n_tm - 1 - tm, reach)
    barrier = pltpu.get_barrier_semaphore()
    answers, complete = ready.at[0], ready.at[1]

    def signal(semaphore, target):
        pl.semaphore_signal(semaphore, inc=1, device_id=target, device_id_type=MESH)

    def tell_rows(semaphore):
        @pl.when(hosting)
        def _():
            for k in sorted(range(1, n_rows), key=lambda k: -min(k, n_rows - k)):
                signal(semaphore, device(0, k))

    for d in range(1, reach + 1):

        @pl.when(exists(d))
        def _(d=d):
            signal(barrier, device(d, 0))

    tell_rows(barrier)
    announced = below + jnp.where(hosting, 0, 1)

    def answer():
        for d in range(1, reach + 1):

            @pl.when(exists(-d))
            def _(d=d):
                signal(ready.at[1 + d], device(-d, 0))

        @pl.when(jnp.logical_not(hosting))
        def _():
            signal(answers, {"tm": tm, "rows": host})

    load_lens = pltpu.make_async_copy(lengths, lens, load_sem.at[1])
    load_lens.start()
    for i, vec in enumerate((gain_one, shift_one, bias_one, gain_two, shift_two, bias_two)):
        pltpu.make_async_copy(vec, vecs.at[i], load_sem.at[2]).start()
    for dx in range(3):
        for i, (source, held) in enumerate(((conv_one, taps_one), (conv_two, taps_two))):
            pltpu.make_async_copy(
                source.at[:, :, dx], held.at[:, :, :, pl.ds(dx * width, width)], load_sem.at[3 + i]
            ).start()
    load_vecs = pltpu.make_async_copy(vecs.at[pl.ds(0, 6)], vecs.at[pl.ds(0, 6)], load_sem.at[2])
    load_one = pltpu.make_async_copy(taps_one, taps_one, load_sem.at[3])
    load_two = pltpu.make_async_copy(taps_two, taps_two, load_sem.at[4])

    def remote(src, dst, send, recv, d, k):
        return pltpu.make_async_remote_copy(
            src_ref=src,
            dst_ref=dst,
            send_sem=send,
            recv_sem=recv,
            device_id=device(d, k),
            device_id_type=MESH,
        )

    class Halo:
        def __init__(self, block, half, passed):
            own, prior = pl.ds(count, count), pl.ds(0, count)
            whole, last, head = pl.ds(1, height), pl.ds(height, 1), pl.ds(1, 1)
            above, below = pl.ds(0, 1), pl.ds(height + 1, 1)

            def copy(f, src, g, dst, d, k):
                sems = halo_send.at[half, d], halo_recv.at[half, d]
                return remote(block.at[f, src], block.at[g, dst], *sems, d, k)

            self.beside = [copy(own, last, own, above, 0, 1), copy(own, head, own, below, 0, -1)]
            halves = [(pl.ds(count + f, 1), pl.ds(f, 1)) for f in range(count)]
            self.onward = [copy(src, whole, dst, whole, 1, 0) for src, dst in halves]
            if passed:
                self.corners = [copy(own, above, prior, above, 1, 0), copy(own, below, prior, below, 1, 0)]
            else:
                self.corners = [copy(own, last, prior, above, 1, 1), copy(own, head, prior, below, 1, -1)]
            edge = block.at[:, pl.ds(0, 1)]
            self.all_beside = remote(edge, edge, halo_send.at[half, 0], halo_recv.at[half, 0], 0, 1)
            front = block.at[prior]
            self.all_onward = remote(front, front, halo_send.at[half, 1], halo_recv.at[half, 1], 0, 1)

        def start_beside(self):
            for copy in self.beside:
                copy.start()

        def start_onward(self, *halves):
            @pl.when(exists(1))
            def _():
                for half in halves:
                    self.onward[half].start()

        def start_corners(self):
            @pl.when(exists(1))
            def _():
                for copy in self.corners:
                    copy.start()

        def wait_onward(self):
            pl.when(exists(-1))(self.all_onward.wait_recv)

        def wait_send(self):
            self.all_beside.wait_send()
            pl.when(exists(1))(self.all_onward.wait_send)

    class Rows:
        def __init__(self, slots, half):
            sems = row_send.at[half], row_recv.at[half]
            self.copies = [
                remote(slots.at[pl.ds(0, 1)], slots.at[pl.ds(k, 1)], *sems, 0, k) for k in range(1, n_rows)
            ]
            others = slots.at[pl.ds(1, n_rows - 1)]
            self.all = remote(others, others, *sems, 0, 1)

        def start(self):
            for k in sorted(range(1, n_rows), key=lambda k: -min(k, n_rows - k)):
                self.copies[k - 1].start()

    class Frames:
        def __init__(self, slots, half):
            sems = tm_send.at[half], tm_recv.at[half]
            self.copies = {
                d: remote(slots.at[pl.ds(0, 1)], slots.at[pl.ds(1 + i, 1)], *sems, d, 0)
                for i, d in enumerate(offsets)
            }
            self.all = {}
            for n in range(reach, 2 * reach + 1):
                others = slots.at[pl.ds(1, n)]
                self.all[n] = remote(others, others, *sems, 0, 1)

        def start(self, *signs):
            for d in sorted(range(1, reach + 1), key=lambda d: -tm_hops(d)):
                for sign in signs:
                    pl.when(exists(sign * d))(self.copies[sign * d].start)

        def wait_recv(self):
            for n in self.all:
                pl.when(below + above == n)(self.all[n].wait_recv)

        def wait_send(self):
            for n in self.all:
                pl.when(below + above == n)(self.all[n].wait_send)

    members = width // GROUPS
    per_block = float(height * cols * members)
    place = lax.rem(lax.broadcasted_iota(jnp.int32, (1, width), 1), members)
    odd = lax.rem(place, 2) == 1
    head = place < 2

    def local_stats(frames_rows):
        totals, squares = [], []
        for rows in frames_rows:
            near = jnp.sum(rows[0].astype(jnp.float32), axis=0, keepdims=True) * (1.0 / cols)
            first_sum = jnp.zeros((cols, width), jnp.float32)
            second_sum = jnp.zeros((cols, width), jnp.float32)
            for values in rows:
                off = values.astype(jnp.float32) - near
                first_sum = first_sum + off
                second_sum = second_sum + off * off
            first_sum = jnp.sum(first_sum, axis=0, keepdims=True)
            second_sum = jnp.sum(second_sum, axis=0, keepdims=True)
            shift = first_sum * (1.0 / (height * cols))
            total = group_total(first_sum + near * float(height * cols), place)
            off = near + shift - total * (1.0 / per_block)
            square = second_sum - first_sum * shift + off * off * float(height * cols)
            totals.append(total)
            squares.append(group_total(square, place))
        return by_place(place, totals + squares)

    def video_sums(slots, inside, shares):
        parts = slots[...]
        merged = []
        for f in range(count):
            total = jnp.sum(jnp.where(inside[f], parts, 0.0), axis=0, keepdims=True)
            total = total + jnp.where(odd, pltpu.roll(total, 1, 1), pltpu.roll(total, width - 1, 1))
            off = parts * (1.0 / per_block) - total * shares[f]
            between = jnp.sum(jnp.where(inside[f], off * off, 0.0), axis=0, keepdims=True) * per_block
            between = pltpu.roll(between, 2, 1) + jnp.where(
                odd, pltpu.roll(between, 3, 1), pltpu.roll(between, 1, 1)
            )
            merged.append(total + jnp.where(head, 0.0, between))
        return jnp.where(odd, merged[1], merged[0])

    def video_stats(slots, held, share):
        parts = slots[...]
        total = jnp.sum(parts, axis=0, keepdims=True)
        mean = total * share * (1.0 / n_rows)
        off = parts * share - mean
        between = jnp.sum(off * off, axis=0, keepdims=True) * held
        var = (total + pltpu.roll(between, 2, 1)) * share * (1.0 / n_rows)
        near = neighbours(jnp.where(head, mean, lax.rsqrt(var + 1e-6)))
        spread = [by_place(place, [near[i - k] for i in range(4)]) for k in range(4)]
        return [(spread[f], spread[count + f]) for f in range(count)]

    column = lax.broadcasted_iota(jnp.int32, (cols, width), 0)

    def convolved(block, stats, gain, shift, taps):
        def active(f, i, moved):
            mean, scale = stats[max(f - count, 0)]
            v = (block[f, i].astype(jnp.float32) - mean) * (scale * gain) + shift
            v = v * (0.5 * jnp.tanh(0.5 * v) + 0.5)
            if i == 0:
                v = jnp.where(row == 0, 0.0, v)
            if i == height + 1:
                v = jnp.where(row == n_rows - 1, 0.0, v)
            if moved:
                moved = jnp.where(column == cols - 1, 0.0, pltpu.roll(v, cols - 1, 0))
                return v.astype(jnp.bfloat16), moved.astype(jnp.bfloat16)
            return v.astype(jnp.bfloat16)

        seen = [[[], [], []] for _ in range(count)]
        moved = [[], []]
        for i in range(height + 2):
            a, b = active(0, i, False), active(1, i, False)
            c, d = active(2, i, i >= 2), active(3, i, i >= 2)
            if i >= 2:
                c, moved_c = c
                d, moved_d = d
                moved[0].append(moved_c)
                moved[1].append(moved_d)
            b = jnp.where(starts[0] < first, b, c)
            seen[0][0].append(jnp.where(starts[0] < first - 1, a, b))
            seen[0][1].append(b)
            seen[0][2].append(c)
            seen[1][0].append(jnp.where(starts[1] > first, d, b))
            seen[1][1].append(jnp.where(starts[1] > first, d, c))
            seen[1][2].append(d)
        right = taps[...].reshape(9 * width, 3 * width)[: 8 * width]
        ninth = taps[2, 2]
        blank = jnp.zeros((width, width), jnp.bfloat16)
        ninth = jnp.concatenate(
            [ninth[:, : 2 * width], jnp.concatenate([blank, ninth[:, 2 * width :]], axis=1)], axis=0
        )
        results = []
        for f in range(count):
            pieces = [
                jnp.concatenate(seen[f][dt][dy : dy + height], axis=0) for dt in range(3) for dy in range(3)
            ]
            wide = jnp.dot(jnp.concatenate(pieces[:8], axis=1), right, preferred_element_type=jnp.float32)
            last = jnp.concatenate([pieces[8], jnp.concatenate(moved[f], axis=0)], axis=1)
            last = jnp.dot(last, ninth, preferred_element_type=jnp.float32)
            rows = []
            for i in range(height):
                y = wide[i * cols : (i + 1) * cols]
                z = last[i * cols : (i + 1) * cols]
                before = pltpu.roll(y[:, :width] + z[:, :width], 1, 0)
                after = pltpu.roll(y[:, 2 * width :], cols - 1, 0)
                rows.append(
                    y[:, width : 2 * width]
                    + z[:, width:]
                    + jnp.where(column == 0, 0.0, before)
                    + jnp.where(column == cols - 1, 0.0, after)
                )
            results.append(rows)
        return results

    def frame_sums(slots):
        parts = slots[...]
        total = jnp.sum(parts, axis=0, keepdims=True)
        off = parts * (1.0 / per_block) - total * (1.0 / (per_block * n_rows))
        between = jnp.sum(off * off, axis=0, keepdims=True) * per_block
        return total + jnp.where(head, 0.0, pltpu.roll(between, 2, 1))

    def frame_stats(slots, inside, shares):
        parts = slots[...]
        per_frame = per_block * n_rows
        stats = []
        for f in range(count):
            total = jnp.sum(jnp.where(inside[f], parts, 0.0), axis=0, keepdims=True)
            mean = group_total(jnp.where(head, total, 0.0), place) * (shares[f] * (1.0 / n_rows))
            off = parts * (1.0 / per_frame) - mean
            between = jnp.sum(jnp.where(inside[f], off * off, 0.0), axis=0, keepdims=True) * per_frame
            var = group_total(jnp.where(head, between, total), place) * (shares[f] * (1.0 / n_rows))
            stats.append((mean, lax.rsqrt(var + 1e-6)))
        return stats

    await_signals(barrier, announced)
    answer()
    load_frames.wait()
    tms_one[pl.ds(0, 1)] = local_stats(
        [[raw[count + f, 1 + i] for i in range(height)] for f in range(count)]
    )
    tm_sums = Frames(tms_one, 0)
    tm_sums.start(-1)

    load_lens.wait()
    starts, stops = [], []
    for f in range(count):
        start = jnp.int32(0)
        stop = jnp.int32(0)
        offset = jnp.int32(0)
        for v in range(videos):
            size = lens[v]
            here = offset <= first + f
            start = jnp.where(here, offset, start)
            stop = jnp.where(here, offset + size, stop)
            offset = offset + size
        starts.append(start)
        stops.append(stop)
    entries = [(stops[f] - starts[f]).astype(jnp.float32) * per_block for f in range(count)]
    shares = [1.0 / jnp.full((1, width), entries[f], jnp.float32) for f in range(count)]
    held = jnp.where(odd, entries[1], entries[0])
    share = jnp.where(odd, shares[1], shares[0])
    slot = lax.broadcasted_iota(jnp.int32, tms_one.shape, 0)
    lane = lax.broadcasted_iota(jnp.int32, tms_one.shape, 1)
    far = (slot + 1) // 2
    home = tm - jnp.where(lax.rem(slot, 2) == 1, far, -far)
    frame = home * count + lax.rem(lane, count)
    known = slot <= len(offsets)
    inside = [known & (frame >= starts[f]) & (frame < stops[f]) for f in range(count)]

    halo_one = Halo(raw, 0, passed=True)
    for d in range(1, reach + 1):

        @pl.when(exists(d))
        def _(d=d):
            pl.semaphore_wait(ready.at[1 + d], 1)
            tm_sums.copies[d].start()

        if d == reach // 2:
            halo_one.start_onward(0)

    halo_one.start_onward(1)

    @pl.when(hosting)
    def _():
        pl.semaphore_wait(answers, n_rows - 1)

    tell_rows(complete)

    @pl.when(jnp.logical_not(hosting))
    def _():
        pl.semaphore_wait(complete, 1)

    halo_one.start_beside()
    tm_sums.wait_recv()
    rows_one[pl.ds(0, 1)] = video_sums(tms_one, inside, shares)
    row_sums = Rows(rows_one, 0)
    row_sums.start()
    halo_one.all_beside.wait_recv()
    halo_one.start_corners()
    load_vecs.wait()
    row_sums.all.wait_recv()
    stats = video_stats(rows_one, held, share)
    halo_one.wait_onward()
    load_one.wait()
    results = convolved(raw, stats, vecs[0:1], vecs[1:2], taps_one)
    results = [[(y + vecs[2:3]).astype(jnp.bfloat16) for y in rows] for rows in results]
    for f in range(count):
        for i in range(height):
            mid[count + f, 1 + i] = results[f][i]
    rows_two[pl.ds(0, 1)] = local_stats(results)
    row_sums_two = Rows(rows_two, 1)
    row_sums_two.start()
    halo_two = Halo(mid, 1, passed=False)
    halo_two.start_beside()
    halo_two.start_corners()
    halo_two.start_onward(0, 1)
    tm_sums.wait_send()
    row_sums.all.wait_send()
    halo_one.wait_send()

    row_sums_two.all.wait_recv()
    tms_two[pl.ds(0, 1)] = frame_sums(rows_two)
    tm_sums_two = Frames(tms_two, 1)
    tm_sums_two.start(-1)
    tm_sums_two.start(1)
    tm_sums_two.wait_recv()
    stats = frame_stats(tms_two, inside, shares)
    halo_two.all_beside.wait_recv()
    halo_two.wait_onward()
    load_two.wait()
    results = convolved(mid, stats, vecs[3:4], vecs[4:5], taps_two)
    for f in range(count):
        for i in range(height):
            out[f, i] = results[f][i] + vecs[5:6] + raw[count + f, 1 + i].astype(jnp.float32)
    tm_sums_two.wait_send()
    row_sums_two.all.wait_send()
    halo_two.wait_send()


def per_device(n_tm, n_rows, *args):
    frames, lengths = args[0], args[1]
    count, height, cols, width = frames.shape
    near = len(tm_offsets(n_tm, count))
    window = -(-(1 + near) // 8) * 8
    block = pltpu.VMEM((2 * count, height + 2, cols, width), jnp.bfloat16)
    taps = pltpu.VMEM((3, 3, width, 3 * width), jnp.bfloat16)
    return pl.pallas_call(
        functools.partial(kernel, n_tm, n_rows),
        out_shape=pltpu.VMEM(frames.shape, jnp.float32),
        in_specs=[pl.BlockSpec(memory_space=pl.ANY)] * len(args),
        out_specs=pl.BlockSpec(memory_space=pltpu.VMEM),
        scratch_shapes=[
            block, block, taps, taps,
            pltpu.VMEM((8, width), jnp.float32),
            pltpu.SMEM(lengths.shape, jnp.int32),
            pltpu.VMEM((n_rows, width), jnp.float32),
            pltpu.VMEM((n_rows, width), jnp.float32),
            pltpu.VMEM((window, width), jnp.float32),
            pltpu.VMEM((window, width), jnp.float32),
            pltpu.SemaphoreType.REGULAR((2 + near // 2,)),
            pltpu.SemaphoreType.DMA((5,)),
            pltpu.SemaphoreType.DMA((2, 2)),
            pltpu.SemaphoreType.DMA((2, 2)),
            pltpu.SemaphoreType.DMA((2,)),
            pltpu.SemaphoreType.DMA((2,)),
            pltpu.SemaphoreType.DMA((2,)),
            pltpu.SemaphoreType.DMA((2,)),
        ],
        compiler_params=pltpu.CompilerParams(
            collective_id=0, has_side_effects=True, vmem_limit_bytes=40 * 1024 * 1024
        ),
        name="residual_block",
    )(*[pltpu.with_memory_space_constraint(a, pltpu.HBM) for a in args])


def solution(mesh):
    placed = (P("tm", "rows", None, None), P(), P(), P(), P(), P(), P(), P(), P(), P())
    return jax.shard_map(
        functools.partial(per_device, mesh.shape["tm"], mesh.shape["rows"]),
        mesh=mesh,
        in_specs=placed,
        out_specs=P("tm", "rows", None, None),
        check_vma=False,
    )
```

```python
import functools

import jax
import jax.numpy as jnp
from jax import lax
from jax.experimental import pallas as pl
from jax.experimental.pallas import tpu as pltpu
from jax.sharding import PartitionSpec as P

GROUPS = 32
MOST = 16
MESH = pl.DeviceIdType.MESH


def tm_offsets(n_tm, count):
    reach = min(-(-(MOST - 1) // count), n_tm - 1)
    return [d for far in range(1, reach + 1) for d in (far, -far)]


def wrapped(index, offset, size):
    return lax.rem(index + (offset + size), size)


def neighbours(row):
    lanes = row.shape[1]
    return {s: pltpu.roll(row, s % lanes, 1) if s else row for s in range(-3, 4)}


def by_place(place, choices):
    picked = choices[-1]
    for i in range(len(choices) - 1):
        picked = jnp.where(place == i, choices[i], picked)
    return picked


def group_total(row, place):
    near = neighbours(row)
    sums = [near[i] + near[i - 1] + (near[i - 2] + near[i - 3]) for i in range(4)]
    return by_place(place, sums)


def await_signals(semaphore, number):
    @pl.when(number > 0)
    def _():
        pl.semaphore_wait(semaphore, number)


def kernel(
    n_tm, n_rows,
    frames, lengths, gain_one, shift_one, conv_one, bias_one, gain_two, shift_two, conv_two, bias_two,
    out,
    raw, mid, taps_one, taps_two, vecs, lens, rows_one, rows_two, tms_one, tms_two,
    ready, load_sem, halo_send, halo_recv, row_send, row_recv, tm_send, tm_recv,
):
    count, height, cols, width = frames.shape
    videos = lengths.shape[0]
    tm = lax.axis_index("tm")
    row = lax.axis_index("rows")
    first = tm * count
    offsets = tm_offsets(n_tm, count)

    load_frames = pltpu.make_async_copy(
        frames, raw.at[pl.ds(count, count), pl.ds(1, height)], load_sem.at[0]
    )
    load_frames.start()

    def exists(d):
        return (tm + d >= 0) & (tm + d < n_tm)

    def device(d, k):
        return {"tm": tm + d, "rows": wrapped(row, k, n_rows)}

    host = n_rows > 1 and 1
    hosting = row == host
    reach = max(offsets)
    below = jnp.minimum(tm, reach)
    above = jnp.minimum(n_tm - 1 - tm, reach)
    barrier = pltpu.get_barrier_semaphore()
    answers, complete = ready.at[0], ready.at[1]

    def signal(semaphore, target):
        pl.semaphore_signal(semaphore, inc=1, device_id=target, device_id_type=MESH)

    def tell_rows(semaphore):
        @pl.when(hosting)
        def _():
            for k in sorted(range(1, n_rows), key=lambda k: -min(k, n_rows - k)):
                signal(semaphore, device(0, k))

    for d in range(1, reach + 1):

        @pl.when(exists(d))
        def _(d=d):
            signal(barrier, device(d, 0))

    tell_rows(barrier)
    announced = below + jnp.where(hosting, 0, 1)

    def answer():
        for d in range(reach, 0, -1):

            @pl.when(exists(-d))
            def _(d=d):
                signal(ready.at[1 + d], device(-d, 0))

        @pl.when(jnp.logical_not(hosting))
        def _():
            signal(answers, {"tm": tm, "rows": host})

    load_lens = pltpu.make_async_copy(lengths, lens, load_sem.at[1])
    load_lens.start()
    for i, vec in enumerate((gain_one, shift_one, bias_one, gain_two, shift_two, bias_two)):
        pltpu.make_async_copy(vec, vecs.at[i], load_sem.at[2]).start()
    for dx in range(3):
        for i, (source, held) in enumerate(((conv_one, taps_one), (conv_two, taps_two))):
            pltpu.make_async_copy(
                source.at[:, :, dx], held.at[:, :, :, pl.ds(dx * width, width)], load_sem.at[3 + i]
            ).start()
    load_vecs = pltpu.make_async_copy(vecs.at[pl.ds(0, 6)], vecs.at[pl.ds(0, 6)], load_sem.at[2])
    load_one = pltpu.make_async_copy(taps_one, taps_one, load_sem.at[3])
    load_two = pltpu.make_async_copy(taps_two, taps_two, load_sem.at[4])

    def remote(src, dst, send, recv, d, k):
        return pltpu.make_async_remote_copy(
            src_ref=src,
            dst_ref=dst,
            send_sem=send,
            recv_sem=recv,
            device_id=device(d, k),
            device_id_type=MESH,
        )

    class Halo:
        def __init__(self, block, half, passed):
            own, prior = pl.ds(count, count), pl.ds(0, count)
            whole, last, head = pl.ds(1, height), pl.ds(height, 1), pl.ds(1, 1)
            above, below = pl.ds(0, 1), pl.ds(height + 1, 1)

            def copy(f, src, g, dst, d, k):
                sems = halo_send.at[half, d], halo_recv.at[half, d]
                return remote(block.at[f, src], block.at[g, dst], *sems, d, k)

            self.beside = [copy(own, last, own, above, 0, 1), copy(own, head, own, below, 0, -1)]
            halves = [(pl.ds(count + f, 1), pl.ds(f, 1)) for f in range(count)]
            self.onward = [copy(src, whole, dst, whole, 1, 0) for src, dst in halves]
            if passed:
                self.corners = [copy(own, above, prior, above, 1, 0), copy(own, below, prior, below, 1, 0)]
            else:
                self.corners = [copy(own, last, prior, above, 1, 1), copy(own, head, prior, below, 1, -1)]
            edge = block.at[:, pl.ds(0, 1)]
            self.all_beside = remote(edge, edge, halo_send.at[half, 0], halo_recv.at[half, 0], 0, 1)
            front = block.at[prior]
            self.all_onward = remote(front, front, halo_send.at[half, 1], halo_recv.at[half, 1], 0, 1)

        def start_beside(self):
            for copy in self.beside:
                copy.start()

        def start_onward(self, *halves):
            @pl.when(exists(1))
            def _():
                for half in halves:
                    self.onward[half].start()

        def start_corners(self):
            @pl.when(exists(1))
            def _():
                for copy in self.corners:
                    copy.start()

        def wait_onward(self):
            pl.when(exists(-1))(self.all_onward.wait_recv)

        def wait_send(self):
            self.all_beside.wait_send()
            pl.when(exists(1))(self.all_onward.wait_send)

    class Rows:
        def __init__(self, slots, half):
            sems = row_send.at[half], row_recv.at[half]
            self.copies = [
                remote(slots.at[pl.ds(0, 1)], slots.at[pl.ds(k, 1)], *sems, 0, k) for k in range(1, n_rows)
            ]
            others = slots.at[pl.ds(1, n_rows - 1)]
            self.all = remote(others, others, *sems, 0, 1)

        def start(self):
            for k in sorted(range(1, n_rows), key=lambda k: -min(k, n_rows - k)):
                self.copies[k - 1].start()

    class Frames:
        def __init__(self, slots, half):
            sems = tm_send.at[half], tm_recv.at[half]
            self.copies = {
                d: remote(slots.at[pl.ds(0, 1)], slots.at[pl.ds(1 + i, 1)], *sems, d, 0)
                for i, d in enumerate(offsets)
            }
            self.all = {}
            for n in range(reach, 2 * reach + 1):
                others = slots.at[pl.ds(1, n)]
                self.all[n] = remote(others, others, *sems, 0, 1)

        def start(self, *signs):
            for d in range(reach, 0, -1):
                for sign in signs:
                    pl.when(exists(sign * d))(self.copies[sign * d].start)

        def wait_recv(self):
            for n in self.all:
                pl.when(below + above == n)(self.all[n].wait_recv)

        def wait_send(self):
            for n in self.all:
                pl.when(below + above == n)(self.all[n].wait_send)

    members = width // GROUPS
    per_block = float(height * cols * members)
    place = lax.rem(lax.broadcasted_iota(jnp.int32, (1, width), 1), members)
    odd = lax.rem(place, 2) == 1
    head = place < 2

    def local_stats(frames_rows):
        totals, squares = [], []
        for rows in frames_rows:
            near = jnp.sum(rows[0].astype(jnp.float32), axis=0, keepdims=True) * (1.0 / cols)
            first_sum = jnp.zeros((cols, width), jnp.float32)
            second_sum = jnp.zeros((cols, width), jnp.float32)
            for values in rows:
                off = values.astype(jnp.float32) - near
                first_sum = first_sum + off
                second_sum = second_sum + off * off
            first_sum = jnp.sum(first_sum, axis=0, keepdims=True)
            second_sum = jnp.sum(second_sum, axis=0, keepdims=True)
            shift = first_sum * (1.0 / (height * cols))
            total = group_total(first_sum + near * float(height * cols), place)
            off = near + shift - total * (1.0 / per_block)
            square = second_sum - first_sum * shift + off * off * float(height * cols)
            totals.append(total)
            squares.append(group_total(square, place))
        return by_place(place, totals + squares)

    def video_sums(slots, inside, shares):
        parts = slots[...]
        merged = []
        for f in range(count):
            total = jnp.sum(jnp.where(inside[f], parts, 0.0), axis=0, keepdims=True)
            total = total + jnp.where(odd, pltpu.roll(total, 1, 1), pltpu.roll(total, width - 1, 1))
            off = parts * (1.0 / per_block) - total * shares[f]
            between = jnp.sum(jnp.where(inside[f], off * off, 0.0), axis=0, keepdims=True) * per_block
            between = pltpu.roll(between, 2, 1) + jnp.where(
                odd, pltpu.roll(between, 3, 1), pltpu.roll(between, 1, 1)
            )
            merged.append(total + jnp.where(head, 0.0, between))
        return jnp.where(odd, merged[1], merged[0])

    def video_stats(slots, held, share):
        parts = slots[...]
        total = jnp.sum(parts, axis=0, keepdims=True)
        mean = total * share * (1.0 / n_rows)
        off = parts * share - mean
        between = jnp.sum(off * off, axis=0, keepdims=True) * held
        var = (total + pltpu.roll(between, 2, 1)) * share * (1.0 / n_rows)
        near = neighbours(jnp.where(head, mean, lax.rsqrt(var + 1e-6)))
        spread = [by_place(place, [near[i - k] for i in range(4)]) for k in range(4)]
        return [(spread[f], spread[count + f]) for f in range(count)]

    column = lax.broadcasted_iota(jnp.int32, (cols, width), 0)

    def convolved(block, stats, gain, shift, taps):
        def active(f, i, moved):
            mean, scale = stats[max(f - count, 0)]
            v = (block[f, i].astype(jnp.float32) - mean) * (scale * gain) + shift
            v = v * (0.5 * jnp.tanh(0.5 * v) + 0.5)
            if i == 0:
                v = jnp.where(row == 0, 0.0, v)
            if i == height + 1:
                v = jnp.where(row == n_rows - 1, 0.0, v)
            if moved:
                moved = jnp.where(column == cols - 1, 0.0, pltpu.roll(v, cols - 1, 0))
                return v.astype(jnp.bfloat16), moved.astype(jnp.bfloat16)
            return v.astype(jnp.bfloat16)

        seen = [[[], [], []] for _ in range(count)]
        moved = [[], []]
        for i in range(height + 2):
            a, b = active(0, i, False), active(1, i, False)
            c, d = active(2, i, i >= 2), active(3, i, i >= 2)
            if i >= 2:
                c, moved_c = c
                d, moved_d = d
                moved[0].append(moved_c)
                moved[1].append(moved_d)
            b = jnp.where(starts[0] < first, b, c)
            seen[0][0].append(jnp.where(starts[0] < first - 1, a, b))
            seen[0][1].append(b)
            seen[0][2].append(c)
            seen[1][0].append(jnp.where(starts[1] > first, d, b))
            seen[1][1].append(jnp.where(starts[1] > first, d, c))
            seen[1][2].append(d)
        right = taps[...].reshape(9 * width, 3 * width)[: 8 * width]
        ninth = taps[2, 2]
        blank = jnp.zeros((width, width), jnp.bfloat16)
        ninth = jnp.concatenate(
            [ninth[:, : 2 * width], jnp.concatenate([blank, ninth[:, 2 * width :]], axis=1)], axis=0
        )
        results = []
        for f in range(count):
            pieces = [
                jnp.concatenate(seen[f][dt][dy : dy + height], axis=0) for dt in range(3) for dy in range(3)
            ]
            wide = jnp.dot(jnp.concatenate(pieces[:8], axis=1), right, preferred_element_type=jnp.float32)
            last = jnp.concatenate([pieces[8], jnp.concatenate(moved[f], axis=0)], axis=1)
            last = jnp.dot(last, ninth, preferred_element_type=jnp.float32)
            rows = []
            for i in range(height):
                y = wide[i * cols : (i + 1) * cols]
                z = last[i * cols : (i + 1) * cols]
                before = pltpu.roll(y[:, :width] + z[:, :width], 1, 0)
                after = pltpu.roll(y[:, 2 * width :], cols - 1, 0)
                rows.append(
                    y[:, width : 2 * width]
                    + z[:, width:]
                    + jnp.where(column == 0, 0.0, before)
                    + jnp.where(column == cols - 1, 0.0, after)
                )
            results.append(rows)
        return results

    def frame_sums(slots):
        parts = slots[...]
        total = jnp.sum(parts, axis=0, keepdims=True)
        off = parts * (1.0 / per_block) - total * (1.0 / (per_block * n_rows))
        between = jnp.sum(off * off, axis=0, keepdims=True) * per_block
        return total + jnp.where(head, 0.0, pltpu.roll(between, 2, 1))

    def frame_stats(slots, inside, shares):
        parts = slots[...]
        per_frame = per_block * n_rows
        stats = []
        for f in range(count):
            total = jnp.sum(jnp.where(inside[f], parts, 0.0), axis=0, keepdims=True)
            mean = group_total(jnp.where(head, total, 0.0), place) * (shares[f] * (1.0 / n_rows))
            off = parts * (1.0 / per_frame) - mean
            between = jnp.sum(jnp.where(inside[f], off * off, 0.0), axis=0, keepdims=True) * per_frame
            var = group_total(jnp.where(head, between, total), place) * (shares[f] * (1.0 / n_rows))
            stats.append((mean, lax.rsqrt(var + 1e-6)))
        return stats

    await_signals(barrier, announced)
    answer()
    load_frames.wait()
    tms_one[pl.ds(0, 1)] = local_stats(
        [[raw[count + f, 1 + i] for i in range(height)] for f in range(count)]
    )
    tm_sums = Frames(tms_one, 0)
    tm_sums.start(-1)

    load_lens.wait()
    starts, stops = [], []
    for f in range(count):
        start = jnp.int32(0)
        stop = jnp.int32(0)
        offset = jnp.int32(0)
        for v in range(videos):
            size = lens[v]
            here = offset <= first + f
            start = jnp.where(here, offset, start)
            stop = jnp.where(here, offset + size, stop)
            offset = offset + size
        starts.append(start)
        stops.append(stop)
    entries = [(stops[f] - starts[f]).astype(jnp.float32) * per_block for f in range(count)]
    shares = [1.0 / jnp.full((1, width), entries[f], jnp.float32) for f in range(count)]
    held = jnp.where(odd, entries[1], entries[0])
    share = jnp.where(odd, shares[1], shares[0])
    slot = lax.broadcasted_iota(jnp.int32, tms_one.shape, 0)
    lane = lax.broadcasted_iota(jnp.int32, tms_one.shape, 1)
    far = (slot + 1) // 2
    home = tm - jnp.where(lax.rem(slot, 2) == 1, far, -far)
    frame = home * count + lax.rem(lane, count)
    known = slot <= len(offsets)
    inside = [known & (frame >= starts[f]) & (frame < stops[f]) for f in range(count)]

    halo_one = Halo(raw, 0, passed=True)
    for d in range(1, reach + 1):

        @pl.when(exists(d))
        def _(d=d):
            pl.semaphore_wait(ready.at[1 + d], 1)
            tm_sums.copies[d].start()

        if d == reach // 2:
            halo_one.start_onward(0)

    halo_one.start_onward(1)

    @pl.when(hosting)
    def _():
        pl.semaphore_wait(answers, n_rows - 1)

    tell_rows(complete)

    @pl.when(jnp.logical_not(hosting))
    def _():
        pl.semaphore_wait(complete, 1)

    halo_one.start_beside()
    tm_sums.wait_recv()
    rows_one[pl.ds(0, 1)] = video_sums(tms_one, inside, shares)
    row_sums = Rows(rows_one, 0)
    row_sums.start()
    halo_one.all_beside.wait_recv()
    halo_one.start_corners()
    load_vecs.wait()
    row_sums.all.wait_recv()
    stats = video_stats(rows_one, held, share)
    halo_one.wait_onward()
    load_one.wait()
    results = convolved(raw, stats, vecs[0:1], vecs[1:2], taps_one)
    results = [[(y + vecs[2:3]).astype(jnp.bfloat16) for y in rows] for rows in results]
    for f in range(count):
        for i in range(height):
            mid[count + f, 1 + i] = results[f][i]
    rows_two[pl.ds(0, 1)] = local_stats(results)
    row_sums_two = Rows(rows_two, 1)
    row_sums_two.start()
    halo_two = Halo(mid, 1, passed=False)
    halo_two.start_beside()
    halo_two.start_corners()
    halo_two.start_onward(0, 1)
    tm_sums.wait_send()
    row_sums.all.wait_send()
    halo_one.wait_send()

    row_sums_two.all.wait_recv()
    tms_two[pl.ds(0, 1)] = frame_sums(rows_two)
    tm_sums_two = Frames(tms_two, 1)
    tm_sums_two.start(-1)
    tm_sums_two.start(1)
    tm_sums_two.wait_recv()
    stats = frame_stats(tms_two, inside, shares)
    halo_two.all_beside.wait_recv()
    halo_two.wait_onward()
    load_two.wait()
    results = convolved(mid, stats, vecs[3:4], vecs[4:5], taps_two)
    for f in range(count):
        for i in range(height):
            out[f, i] = results[f][i] + vecs[5:6] + raw[count + f, 1 + i].astype(jnp.float32)
    tm_sums_two.wait_send()
    row_sums_two.all.wait_send()
    halo_two.wait_send()


def per_device(n_tm, n_rows, *args):
    frames, lengths = args[0], args[1]
    count, height, cols, width = frames.shape
    near = len(tm_offsets(n_tm, count))
    window = -(-(1 + near) // 8) * 8
    block = pltpu.VMEM((2 * count, height + 2, cols, width), jnp.bfloat16)
    taps = pltpu.VMEM((3, 3, width, 3 * width), jnp.bfloat16)
    return pl.pallas_call(
        functools.partial(kernel, n_tm, n_rows),
        out_shape=pltpu.VMEM(frames.shape, jnp.float32),
        in_specs=[pl.BlockSpec(memory_space=pl.ANY)] * len(args),
        out_specs=pl.BlockSpec(memory_space=pltpu.VMEM),
        scratch_shapes=[
            block, block, taps, taps,
            pltpu.VMEM((8, width), jnp.float32),
            pltpu.SMEM(lengths.shape, jnp.int32),
            pltpu.VMEM((n_rows, width), jnp.float32),
            pltpu.VMEM((n_rows, width), jnp.float32),
            pltpu.VMEM((window, width), jnp.float32),
            pltpu.VMEM((window, width), jnp.float32),
            pltpu.SemaphoreType.REGULAR((2 + near // 2,)),
            pltpu.SemaphoreType.DMA((5,)),
            pltpu.SemaphoreType.DMA((2, 2)),
            pltpu.SemaphoreType.DMA((2, 2)),
            pltpu.SemaphoreType.DMA((2,)),
            pltpu.SemaphoreType.DMA((2,)),
            pltpu.SemaphoreType.DMA((2,)),
            pltpu.SemaphoreType.DMA((2,)),
        ],
        compiler_params=pltpu.CompilerParams(
            collective_id=0, has_side_effects=True, vmem_limit_bytes=40 * 1024 * 1024
        ),
        name="residual_block",
    )(*[pltpu.with_memory_space_constraint(a, pltpu.HBM) for a in args])


def solution(mesh):
    placed = (P("tm", "rows", None, None), P(), P(), P(), P(), P(), P(), P(), P(), P())
    return jax.shard_map(
        functools.partial(per_device, mesh.shape["tm"], mesh.shape["rows"]),
        mesh=mesh,
        in_specs=placed,
        out_specs=P("tm", "rows", None, None),
        check_vma=False,
    )
```

```python
import functools

import jax
import jax.numpy as jnp
from jax import lax
from jax.experimental import pallas as pl
from jax.experimental.pallas import tpu as pltpu
from jax.sharding import PartitionSpec as P

GROUPS = 32
MOST = 16
MESH = pl.DeviceIdType.MESH


def tm_offsets(n_tm, count):
    reach = min(-(-(MOST - 1) // count), n_tm - 1)
    return [d for far in range(1, reach + 1) for d in (far, -far)]


def tm_hops(d):
    return abs(d) // 4 + min(abs(d) % 4, 4 - abs(d) % 4)


def wrapped(index, offset, size):
    return lax.rem(index + (offset + size), size)


def neighbours(row):
    lanes = row.shape[1]
    return {s: pltpu.roll(row, s % lanes, 1) if s else row for s in range(-3, 4)}


def by_place(place, choices):
    picked = choices[-1]
    for i in range(len(choices) - 1):
        picked = jnp.where(place == i, choices[i], picked)
    return picked


def group_total(row, place):
    near = neighbours(row)
    sums = [near[i] + near[i - 1] + (near[i - 2] + near[i - 3]) for i in range(4)]
    return by_place(place, sums)


def await_signals(semaphore, number):
    @pl.when(number > 0)
    def _():
        pl.semaphore_wait(semaphore, number)


def kernel(
    n_tm, n_rows,
    frames, lengths, gain_one, shift_one, conv_one, bias_one, gain_two, shift_two, conv_two, bias_two,
    out,
    raw, mid, taps_one, taps_two, vecs, lens, rows_one, rows_two, tms_one, tms_two,
    ready, load_sem, halo_send, halo_recv, row_send, row_recv, tm_send, tm_recv,
):
    count, height, cols, width = frames.shape
    videos = lengths.shape[0]
    tm = lax.axis_index("tm")
    row = lax.axis_index("rows")
    first = tm * count
    offsets = tm_offsets(n_tm, count)

    load_frames = pltpu.make_async_copy(
        frames, raw.at[pl.ds(count, count), pl.ds(1, height)], load_sem.at[0]
    )
    load_frames.start()

    def exists(d):
        return (tm + d >= 0) & (tm + d < n_tm)

    def device(d, k):
        return {"tm": tm + d, "rows": wrapped(row, k, n_rows)}

    host = n_rows > 1 and 1
    hosting = row == host
    reach = max(offsets)
    below = jnp.minimum(tm, reach)
    above = jnp.minimum(n_tm - 1 - tm, reach)
    barrier = pltpu.get_barrier_semaphore()
    answers, complete = ready.at[0], ready.at[1]

    def signal(semaphore, target):
        pl.semaphore_signal(semaphore, inc=1, device_id=target, device_id_type=MESH)

    def tell_rows(semaphore):
        @pl.when(hosting)
        def _():
            for k in sorted(range(1, n_rows), key=lambda k: -min(k, n_rows - k)):
                signal(semaphore, device(0, k))

    for d in range(1, reach + 1):

        @pl.when(exists(d))
        def _(d=d):
            signal(barrier, device(d, 0))

    tell_rows(barrier)
    announced = below + jnp.where(hosting, 0, 1)

    def answer():
        for d in range(reach, 0, -1):

            @pl.when(exists(-d))
            def _(d=d):
                signal(ready.at[1 + d], device(-d, 0))

        @pl.when(jnp.logical_not(hosting))
        def _():
            signal(answers, {"tm": tm, "rows": host})

    load_lens = pltpu.make_async_copy(lengths, lens, load_sem.at[1])
    load_lens.start()
    for i, vec in enumerate((gain_one, shift_one, bias_one, gain_two, shift_two, bias_two)):
        pltpu.make_async_copy(vec, vecs.at[i], load_sem.at[2]).start()
    for dx in range(3):
        for i, (source, held) in enumerate(((conv_one, taps_one), (conv_two, taps_two))):
            pltpu.make_async_copy(
                source.at[:, :, dx], held.at[:, :, :, pl.ds(dx * width, width)], load_sem.at[3 + i]
            ).start()
    load_vecs = pltpu.make_async_copy(vecs.at[pl.ds(0, 6)], vecs.at[pl.ds(0, 6)], load_sem.at[2])
    load_one = pltpu.make_async_copy(taps_one, taps_one, load_sem.at[3])
    load_two = pltpu.make_async_copy(taps_two, taps_two, load_sem.at[4])

    def remote(src, dst, send, recv, d, k):
        return pltpu.make_async_remote_copy(
            src_ref=src,
            dst_ref=dst,
            send_sem=send,
            recv_sem=recv,
            device_id=device(d, k),
            device_id_type=MESH,
        )

    class Halo:
        def __init__(self, block, half, passed):
            own, prior = pl.ds(count, count), pl.ds(0, count)
            whole, last, head = pl.ds(1, height), pl.ds(height, 1), pl.ds(1, 1)
            above, below = pl.ds(0, 1), pl.ds(height + 1, 1)

            def copy(f, src, g, dst, d, k):
                sems = halo_send.at[half, d], halo_recv.at[half, d]
                return remote(block.at[f, src], block.at[g, dst], *sems, d, k)

            self.beside = [copy(own, last, own, above, 0, 1), copy(own, head, own, below, 0, -1)]
            halves = [(pl.ds(count + f, 1), pl.ds(f, 1)) for f in range(count)]
            self.onward = [copy(src, whole, dst, whole, 1, 0) for src, dst in halves]
            if passed:
                self.corners = [copy(own, above, prior, above, 1, 0), copy(own, below, prior, below, 1, 0)]
            else:
                self.corners = [copy(own, last, prior, above, 1, 1), copy(own, head, prior, below, 1, -1)]
            edge = block.at[:, pl.ds(0, 1)]
            self.all_beside = remote(edge, edge, halo_send.at[half, 0], halo_recv.at[half, 0], 0, 1)
            front = block.at[prior]
            self.all_onward = remote(front, front, halo_send.at[half, 1], halo_recv.at[half, 1], 0, 1)

        def start_beside(self):
            for copy in self.beside:
                copy.start()

        def start_onward(self, *halves):
            @pl.when(exists(1))
            def _():
                for half in halves:
                    self.onward[half].start()

        def start_corners(self):
            @pl.when(exists(1))
            def _():
                for copy in self.corners:
                    copy.start()

        def wait_onward(self):
            pl.when(exists(-1))(self.all_onward.wait_recv)

        def wait_send(self):
            self.all_beside.wait_send()
            pl.when(exists(1))(self.all_onward.wait_send)

    class Rows:
        def __init__(self, slots, half):
            sems = row_send.at[half], row_recv.at[half]
            self.copies = [
                remote(slots.at[pl.ds(0, 1)], slots.at[pl.ds(k, 1)], *sems, 0, k) for k in range(1, n_rows)
            ]
            others = slots.at[pl.ds(1, n_rows - 1)]
            self.all = remote(others, others, *sems, 0, 1)

        def start(self):
            for k in sorted(range(1, n_rows), key=lambda k: -min(k, n_rows - k)):
                self.copies[k - 1].start()

    class Frames:
        def __init__(self, slots, half):
            sems = tm_send.at[half], tm_recv.at[half]
            self.copies = {
                d: remote(slots.at[pl.ds(0, 1)], slots.at[pl.ds(1 + i, 1)], *sems, d, 0)
                for i, d in enumerate(offsets)
            }
            self.all = {}
            for n in range(reach, 2 * reach + 1):
                others = slots.at[pl.ds(1, n)]
                self.all[n] = remote(others, others, *sems, 0, 1)

        def start(self, *signs):
            for d in sorted(range(1, reach + 1), key=lambda d: -tm_hops(d)):
                for sign in signs:
                    pl.when(exists(sign * d))(self.copies[sign * d].start)

        def wait_recv(self):
            for n in self.all:
                pl.when(below + above == n)(self.all[n].wait_recv)

        def wait_send(self):
            for n in self.all:
                pl.when(below + above == n)(self.all[n].wait_send)

    members = width // GROUPS
    per_block = float(height * cols * members)
    place = lax.rem(lax.broadcasted_iota(jnp.int32, (1, width), 1), members)
    odd = lax.rem(place, 2) == 1
    head = place < 2

    def local_stats(frames_rows):
        totals, squares = [], []
        for rows in frames_rows:
            near = jnp.sum(rows[0].astype(jnp.float32), axis=0, keepdims=True) * (1.0 / cols)
            first_sum = jnp.zeros((cols, width), jnp.float32)
            second_sum = jnp.zeros((cols, width), jnp.float32)
            for values in rows:
                off = values.astype(jnp.float32) - near
                first_sum = first_sum + off
                second_sum = second_sum + off * off
            first_sum = jnp.sum(first_sum, axis=0, keepdims=True)
            second_sum = jnp.sum(second_sum, axis=0, keepdims=True)
            shift = first_sum * (1.0 / (height * cols))
            total = group_total(first_sum + near * float(height * cols), place)
            off = near + shift - total * (1.0 / per_block)
            square = second_sum - first_sum * shift + off * off * float(height * cols)
            totals.append(total)
            squares.append(group_total(square, place))
        return by_place(place, totals + squares)

    def video_sums(slots, inside, shares):
        parts = slots[...]
        merged = []
        for f in range(count):
            total = jnp.sum(jnp.where(inside[f], parts, 0.0), axis=0, keepdims=True)
            total = total + jnp.where(odd, pltpu.roll(total, 1, 1), pltpu.roll(total, width - 1, 1))
            off = parts * (1.0 / per_block) - total * shares[f]
            between = jnp.sum(jnp.where(inside[f], off * off, 0.0), axis=0, keepdims=True) * per_block
            between = pltpu.roll(between, 2, 1) + jnp.where(
                odd, pltpu.roll(between, 3, 1), pltpu.roll(between, 1, 1)
            )
            merged.append(total + jnp.where(head, 0.0, between))
        return jnp.where(odd, merged[1], merged[0])

    def video_stats(slots, held, share):
        parts = slots[...]
        total = jnp.sum(parts, axis=0, keepdims=True)
        mean = total * share * (1.0 / n_rows)
        off = parts * share - mean
        between = jnp.sum(off * off, axis=0, keepdims=True) * held
        var = (total + pltpu.roll(between, 2, 1)) * share * (1.0 / n_rows)
        near = neighbours(jnp.where(head, mean, lax.rsqrt(var + 1e-6)))
        spread = [by_place(place, [near[i - k] for i in range(4)]) for k in range(4)]
        return [(spread[f], spread[count + f]) for f in range(count)]

    column = lax.broadcasted_iota(jnp.int32, (cols, width), 0)

    def convolved(block, stats, gain, shift, taps):
        def active(f, i, moved):
            mean, scale = stats[max(f - count, 0)]
            v = (block[f, i].astype(jnp.float32) - mean) * (scale * gain) + shift
            v = v * (0.5 * jnp.tanh(0.5 * v) + 0.5)
            if i == 0:
                v = jnp.where(row == 0, 0.0, v)
            if i == height + 1:
                v = jnp.where(row == n_rows - 1, 0.0, v)
            if moved:
                moved = jnp.where(column == cols - 1, 0.0, pltpu.roll(v, cols - 1, 0))
                return v.astype(jnp.bfloat16), moved.astype(jnp.bfloat16)
            return v.astype(jnp.bfloat16)

        seen = [[[], [], []] for _ in range(count)]
        moved = [[], []]
        for i in range(height + 2):
            a, b = active(0, i, False), active(1, i, False)
            c, d = active(2, i, i >= 2), active(3, i, i >= 2)
            if i >= 2:
                c, moved_c = c
                d, moved_d = d
                moved[0].append(moved_c)
                moved[1].append(moved_d)
            b = jnp.where(starts[0] < first, b, c)
            seen[0][0].append(jnp.where(starts[0] < first - 1, a, b))
            seen[0][1].append(b)
            seen[0][2].append(c)
            seen[1][0].append(jnp.where(starts[1] > first, d, b))
            seen[1][1].append(jnp.where(starts[1] > first, d, c))
            seen[1][2].append(d)
        right = taps[...].reshape(9 * width, 3 * width)[: 8 * width]
        ninth = taps[2, 2]
        blank = jnp.zeros((width, width), jnp.bfloat16)
        ninth = jnp.concatenate(
            [ninth[:, : 2 * width], jnp.concatenate([blank, ninth[:, 2 * width :]], axis=1)], axis=0
        )
        results = []
        for f in range(count):
            pieces = [
                jnp.concatenate(seen[f][dt][dy : dy + height], axis=0) for dt in range(3) for dy in range(3)
            ]
            wide = jnp.dot(jnp.concatenate(pieces[:8], axis=1), right, preferred_element_type=jnp.float32)
            last = jnp.concatenate([pieces[8], jnp.concatenate(moved[f], axis=0)], axis=1)
            last = jnp.dot(last, ninth, preferred_element_type=jnp.float32)
            rows = []
            for i in range(height):
                y = wide[i * cols : (i + 1) * cols]
                z = last[i * cols : (i + 1) * cols]
                before = pltpu.roll(y[:, :width] + z[:, :width], 1, 0)
                after = pltpu.roll(y[:, 2 * width :], cols - 1, 0)
                rows.append(
                    y[:, width : 2 * width]
                    + z[:, width:]
                    + jnp.where(column == 0, 0.0, before)
                    + jnp.where(column == cols - 1, 0.0, after)
                )
            results.append(rows)
        return results

    def frame_sums(slots):
        parts = slots[...]
        total = jnp.sum(parts, axis=0, keepdims=True)
        off = parts * (1.0 / per_block) - total * (1.0 / (per_block * n_rows))
        between = jnp.sum(off * off, axis=0, keepdims=True) * per_block
        return total + jnp.where(head, 0.0, pltpu.roll(between, 2, 1))

    def frame_stats(slots, inside, shares):
        parts = slots[...]
        per_frame = per_block * n_rows
        stats = []
        for f in range(count):
            total = jnp.sum(jnp.where(inside[f], parts, 0.0), axis=0, keepdims=True)
            mean = group_total(jnp.where(head, total, 0.0), place) * (shares[f] * (1.0 / n_rows))
            off = parts * (1.0 / per_frame) - mean
            between = jnp.sum(jnp.where(inside[f], off * off, 0.0), axis=0, keepdims=True) * per_frame
            var = group_total(jnp.where(head, between, total), place) * (shares[f] * (1.0 / n_rows))
            stats.append((mean, lax.rsqrt(var + 1e-6)))
        return stats

    await_signals(barrier, announced)
    answer()
    load_frames.wait()
    tms_one[pl.ds(0, 1)] = local_stats(
        [[raw[count + f, 1 + i] for i in range(height)] for f in range(count)]
    )
    tm_sums = Frames(tms_one, 0)
    tm_sums.start(-1)

    load_lens.wait()
    starts, stops = [], []
    for f in range(count):
        start = jnp.int32(0)
        stop = jnp.int32(0)
        offset = jnp.int32(0)
        for v in range(videos):
            size = lens[v]
            here = offset <= first + f
            start = jnp.where(here, offset, start)
            stop = jnp.where(here, offset + size, stop)
            offset = offset + size
        starts.append(start)
        stops.append(stop)
    entries = [(stops[f] - starts[f]).astype(jnp.float32) * per_block for f in range(count)]
    shares = [1.0 / jnp.full((1, width), entries[f], jnp.float32) for f in range(count)]
    held = jnp.where(odd, entries[1], entries[0])
    share = jnp.where(odd, shares[1], shares[0])
    slot = lax.broadcasted_iota(jnp.int32, tms_one.shape, 0)
    lane = lax.broadcasted_iota(jnp.int32, tms_one.shape, 1)
    far = (slot + 1) // 2
    home = tm - jnp.where(lax.rem(slot, 2) == 1, far, -far)
    frame = home * count + lax.rem(lane, count)
    known = slot <= len(offsets)
    inside = [known & (frame >= starts[f]) & (frame < stops[f]) for f in range(count)]

    halo_one = Halo(raw, 0, passed=True)
    for d in range(1, reach + 1):

        @pl.when(exists(d))
        def _(d=d):
            pl.semaphore_wait(ready.at[1 + d], 1)
            tm_sums.copies[d].start()

        if d == reach // 2:
            halo_one.start_onward(0)

    halo_one.start_onward(1)

    @pl.when(hosting)
    def _():
        pl.semaphore_wait(answers, n_rows - 1)

    tell_rows(complete)

    @pl.when(jnp.logical_not(hosting))
    def _():
        pl.semaphore_wait(complete, 1)

    halo_one.start_beside()
    tm_sums.wait_recv()
    rows_one[pl.ds(0, 1)] = video_sums(tms_one, inside, shares)
    row_sums = Rows(rows_one, 0)
    row_sums.start()
    halo_one.all_beside.wait_recv()
    halo_one.start_corners()
    load_vecs.wait()
    row_sums.all.wait_recv()
    stats = video_stats(rows_one, held, share)
    halo_one.wait_onward()
    load_one.wait()
    results = convolved(raw, stats, vecs[0:1], vecs[1:2], taps_one)
    results = [[(y + vecs[2:3]).astype(jnp.bfloat16) for y in rows] for rows in results]
    for f in range(count):
        for i in range(height):
            mid[count + f, 1 + i] = results[f][i]
    rows_two[pl.ds(0, 1)] = local_stats(results)
    row_sums_two = Rows(rows_two, 1)
    row_sums_two.start()
    halo_two = Halo(mid, 1, passed=False)
    halo_two.start_beside()
    halo_two.start_corners()
    halo_two.start_onward(0, 1)
    tm_sums.wait_send()
    row_sums.all.wait_send()
    halo_one.wait_send()

    row_sums_two.all.wait_recv()
    tms_two[pl.ds(0, 1)] = frame_sums(rows_two)
    tm_sums_two = Frames(tms_two, 1)
    tm_sums_two.start(-1)
    tm_sums_two.start(1)
    tm_sums_two.wait_recv()
    stats = frame_stats(tms_two, inside, shares)
    halo_two.all_beside.wait_recv()
    halo_two.wait_onward()
    load_two.wait()
    results = convolved(mid, stats, vecs[3:4], vecs[4:5], taps_two)
    for f in range(count):
        for i in range(height):
            out[f, i] = results[f][i] + vecs[5:6] + raw[count + f, 1 + i].astype(jnp.float32)
    tm_sums_two.wait_send()
    row_sums_two.all.wait_send()
    halo_two.wait_send()


def per_device(n_tm, n_rows, *args):
    frames, lengths = args[0], args[1]
    count, height, cols, width = frames.shape
    near = len(tm_offsets(n_tm, count))
    window = -(-(1 + near) // 8) * 8
    block = pltpu.VMEM((2 * count, height + 2, cols, width), jnp.bfloat16)
    taps = pltpu.VMEM((3, 3, width, 3 * width), jnp.bfloat16)
    return pl.pallas_call(
        functools.partial(kernel, n_tm, n_rows),
        out_shape=pltpu.VMEM(frames.shape, jnp.float32),
        in_specs=[pl.BlockSpec(memory_space=pl.ANY)] * len(args),
        out_specs=pl.BlockSpec(memory_space=pltpu.VMEM),
        scratch_shapes=[
            block, block, taps, taps,
            pltpu.VMEM((8, width), jnp.float32),
            pltpu.SMEM(lengths.shape, jnp.int32),
            pltpu.VMEM((n_rows, width), jnp.float32),
            pltpu.VMEM((n_rows, width), jnp.float32),
            pltpu.VMEM((window, width), jnp.float32),
            pltpu.VMEM((window, width), jnp.float32),
            pltpu.SemaphoreType.REGULAR((2 + near // 2,)),
            pltpu.SemaphoreType.DMA((5,)),
            pltpu.SemaphoreType.DMA((2, 2)),
            pltpu.SemaphoreType.DMA((2, 2)),
            pltpu.SemaphoreType.DMA((2,)),
            pltpu.SemaphoreType.DMA((2,)),
            pltpu.SemaphoreType.DMA((2,)),
            pltpu.SemaphoreType.DMA((2,)),
        ],
        compiler_params=pltpu.CompilerParams(
            collective_id=0, has_side_effects=True, vmem_limit_bytes=40 * 1024 * 1024
        ),
        name="residual_block",
    )(*[pltpu.with_memory_space_constraint(a, pltpu.HBM) for a in args])


def solution(mesh):
    placed = (P("tm", "rows", None, None), P(), P(), P(), P(), P(), P(), P(), P(), P())
    return jax.shard_map(
        functools.partial(per_device, mesh.shape["tm"], mesh.shape["rows"]),
        mesh=mesh,
        in_specs=placed,
        out_specs=P("tm", "rows", None, None),
        check_vma=False,
    )
```
